32 devices in a mesh: groups: 2 (over y), orient: 4 (over z), img: 2 (over x), brick: 2 (over core).
Axes of the slice: x: 2, y: 2, z: 4, core: 2. Of those that a mesh axis runs over, the one named last changes fastest.
Arguments:
- images: bfloat16 [1024, 4096], P(('groups', 'orient', 'img', 'brick')), parts along dimension 0, may hold values from -8 to 8
- offsets: int32 [1024, 2], P('groups'), parts along dimension 0, may hold values from -6 to 6
- slices: bfloat16 [2048, 4096], P(('groups', 'orient')), parts along dimension 0, may hold values from -3 to 3
- seg_map: int32 [8192, 1], replicated, may hold values from 0 to 15; in each aligned block of 512 rows (0 to 511, 512 to 1023, ...) at most 64 rows name the same one
- interp: int32 [16, 8, 256, 256], P(('orient', 'img', 'brick')), may hold values from 0 to 4095
Outputs:
- brick_values: float32 [32, 2, 256], P(('groups', 'orient', 'img', 'brick')), parts along dimension 0
- brick_weight: float32 [32, 256], P(('groups', 'orient', 'img', 'brick')), parts along dimension 0
The draws below stay inside these ranges and needn't reach their ends.
There are 2 independent parts, one for each index of `groups`. The reference program is written for one: setup_inputs(seed, part) draws one part's arguments, and reference() takes and returns one part's arrays. A program takes and returns all parts, laid end to end along the dimension named above; an argument that names none is the same for every part. Nothing has to cross between parts.
Inputs may be any that keep to these rules, and one draw needn't show every extreme that they name: `seg_map`: in each aligned block of 512 rows no brick is named by more than 64 rows; in every draw some block names some brick exactly 64 times.
All inputs are finite; a program needn't handle non-finite values.
Results may differ from the reference program's by a relative error of at most 0.019.
Values may be sent and summed in bfloat16 or wider, within the bound.
A program may use at most 64 MiB of HBM per device.

```python
import math
import jax
import jax.numpy as jnp
import numpy as np
from jax import lax

K = 2048
SHIFTS = 16
SEG = 256
VOX = 256
NIMG = 512
ORIENT = 1024
NSEG = 8
NBRICK = 16
SEG_ROWS = 512
CAP = 64
N_ORIENT = 4
N_IMG = 2
N_BRICK = 2


def offsets_law(key):
    return jax.random.randint(jax.random.fold_in(key, 7), (NIMG, 2), -6, 7).astype(jnp.int32)


def slices_law(key):
    base = jax.random.normal(jax.random.fold_in(key, 11), (ORIENT, 2 * K), jnp.float32)
    values = jnp.clip(0.5 * base, -3.0, 3.0)
    chosen = jax.random.permutation(jax.random.fold_in(key, 13), ORIENT)[:6]
    values = values.at[chosen[3:]].set(1.015 * values[chosen[:3]])
    return values


def draw_offsets(key, part):
    return offsets_law(key)


def draw_slices(key, part):
    return slices_law(key).astype(jnp.bfloat16)


def draw_images(key, part):
    values = jnp.clip(jax.random.normal(jax.random.fold_in(key, 17), (NIMG, 2 * K), jnp.float32), -6.0, 6.0)
    strength = jnp.array([2.5, 2.75, 3.0], jnp.float32)[:, None]
    slices = slices_law(key)
    chosen = jax.random.permutation(jax.random.fold_in(key, 13), ORIENT)[:3]
    targets = jax.random.permutation(jax.random.fold_in(key, 19), NIMG)[:3]
    pick_shift = jax.random.randint(jax.random.fold_in(key, 23), (3,), 0, SHIFTS)
    chosen_offsets = offsets_law(key)[targets]
    shift_x = chosen_offsets[:, 0] + pick_shift % 4 - 2
    shift_y = chosen_offsets[:, 1] + pick_shift // 4 - 2
    coef_index = jnp.arange(K, dtype=jnp.int32)
    column_freq = coef_index % 64 - 32
    row_freq = coef_index // 64
    phase_index = jnp.mod(shift_x[:, None] * column_freq[None, :] + shift_y[:, None] * row_freq[None, :], 64)
    angle = phase_index.astype(jnp.float32) * (2.0 * jnp.pi / 64.0)
    slice_real = slices[chosen, :K]
    slice_imag = slices[chosen, K:]
    real_part = strength * (slice_real * jnp.cos(angle) - slice_imag * jnp.sin(angle))
    imag_part = strength * (slice_real * jnp.sin(angle) + slice_imag * jnp.cos(angle))
    values = values.at[targets].set(jnp.concatenate([real_part, imag_part], axis=1))
    return jnp.clip(values, -8.0, 8.0).astype(jnp.bfloat16)


def touch_ends(drawn, stream_key, low, largest):
    index_at = [jax.random.randint(jax.random.fold_in(stream_key, axis), (), 0, length) for axis, length in enumerate(drawn.shape)]
    longest = drawn.shape.index(max(drawn.shape))
    next_to = index_at[:longest] + [(index_at[longest] + 1) % drawn.shape[longest]] + index_at[longest + 1:]
    return drawn.at[tuple(index_at)].set(low).at[tuple(next_to)].set(largest)


def assign_block(own_key, own, number, rows, count, top, most, lean):
    sequence = jax.random.permutation(own_key, count)
    crowded, ordinary = shares(count, rows * top, most, lean, True), shares(count, rows * top, most, lean, False)
    places = jnp.arange(count)

    def named(sizes, rotation):
        used = int((sizes > 0).sum())
        fixed = max(1, used // 4)
        moved = fixed + (places - fixed + rotation * (used - fixed)) % max(1, count - fixed)
        return jnp.zeros((count,), jnp.int32).at[sequence[jnp.where(places < fixed, places, moved)]].set(jnp.asarray(sizes, jnp.int32))

    sizes = jnp.where(number % 4 == 0, named(crowded, number // 4), named(ordinary, number - number // 4 - 1))
    mixed = jax.random.permutation(jax.random.fold_in(own, 3), count)
    donor, sink = mixed[0:count // 2 * 2:2], mixed[1:count // 2 * 2:2]
    slack = jnp.minimum(sizes[donor] - 1, most - sizes[sink]) // 2
    slack = jnp.where((donor == sequence[0]) | (sink == sequence[0]) | (sizes[sink] == 0), 0, jnp.maximum(slack, 0))
    moved = jax.random.randint(jax.random.fold_in(own, 4), (count // 2,), 0, 1 << 20) % (slack + 1)
    sizes = sizes.at[donor].add(-moved).at[sink].add(moved)
    items = jnp.searchsorted(jnp.cumsum(sizes), jnp.arange(rows * top), side="right").astype(jnp.int32)
    listing = items.reshape(top, rows).T
    listing = listing[jax.random.permutation(jax.random.fold_in(own, 1), rows)]
    rotation = jax.random.randint(jax.random.fold_in(own, 2), (rows, 1), 0, top)
    return jnp.take_along_axis(listing, (jnp.arange(top)[None, :] + rotation) % top, axis=1)


def shares(number_of, total, bound, slope, full):
    loads = [(1 << 20) // math.isqrt(grade ** slope) + 1 for grade in range(1, number_of + 1)]
    largest = bound if full else min(bound, max(-(-total // number_of), total * loads[0] // sum(loads)))
    least = 1 if total - largest >= number_of - 1 else 0
    counts, rest = [largest] + [least] * (number_of - 1), total - largest - least * (number_of - 1)
    while rest > 0:
        free = [i for i in range(1, number_of) if counts[i] < largest] or [i for i in range(1, number_of) if counts[i] < bound]
        whole, left = sum([loads[i] for i in free]), rest
        for i in free:
            addition = min(bound - counts[i], max(1, left * loads[i] // whole), rest)
            counts[i] = counts[i] + addition
            rest = rest - addition
    return np.array(counts)


def setup_inputs(seed: int = 0, part: int = 0) -> dict:
    seeds = jax.random.split(jax.random.key(seed), 6)
    part_keys = jax.random.split(jax.random.fold_in(seeds[5], part), 6)
    images = draw_images(jax.random.fold_in(jax.random.fold_in(seeds[5], part), 71), part)
    offsets = draw_offsets(jax.random.fold_in(jax.random.fold_in(seeds[5], part), 71), part)
    slices = draw_slices(jax.random.fold_in(jax.random.fold_in(seeds[5], part), 71), part)
    seg_map_keys = jax.random.split(jax.random.fold_in(seeds[3], 1), (ORIENT * NSEG) // SEG_ROWS)
    seg_map_turns = jax.random.permutation(jax.random.fold_in(seeds[3], 3), (ORIENT * NSEG) // SEG_ROWS)
    seg_map = jax.vmap(lambda own, number: assign_block(jax.random.fold_in(seeds[3], 2), own, number, SEG_ROWS, NBRICK, 1, CAP, 2))(seg_map_keys, seg_map_turns).reshape((ORIENT * NSEG, 1))
    interp = touch_ends(jax.random.randint(seeds[4], (NBRICK, NSEG, SEG, VOX), 0, 4096), jax.random.fold_in(seeds[4], 1), 0, 4095).astype(jnp.int32)
    return dict(images=images, offsets=offsets, slices=slices, seg_map=seg_map, interp=interp)


frame_side = 64
interp_scale = 1.0 / 256.0


def shift_images(image_rows, image_offsets):
    row_count = image_rows.shape[0]
    coeffs = image_rows.shape[1] // 2
    coef_index = jnp.arange(coeffs, dtype=jnp.int32)
    column_freq = coef_index % frame_side - frame_side // 2
    row_freq = coef_index // frame_side
    shift_index = jnp.arange(SHIFTS, dtype=jnp.int32)
    shift_x = image_offsets[:, 0][:, None] + (shift_index % 4 - 2)[None, :]
    shift_y = image_offsets[:, 1][:, None] + (shift_index // 4 - 2)[None, :]
    phase_index = jnp.mod(shift_x[:, :, None] * column_freq[None, None, :] + shift_y[:, :, None] * row_freq[None, None, :], frame_side)
    angle = phase_index.astype(jnp.float32) * (2.0 * jnp.pi / frame_side)
    cosine = jnp.cos(angle)
    sine = jnp.sin(angle)
    real_part = image_rows[:, :coeffs].astype(jnp.float32)[:, None, :]
    imag_part = image_rows[:, coeffs:].astype(jnp.float32)[:, None, :]
    out_real = real_part * cosine + imag_part * sine
    out_imag = imag_part * cosine - real_part * sine
    joined = jnp.concatenate([out_real, out_imag], axis=-1).astype(jnp.bfloat16)
    return joined.reshape(row_count * SHIFTS, 2 * coeffs)


def reference(images, offsets, slices, seg_map, interp):
    inv_noise = 100.0 / K
    group_count = N_IMG * N_BRICK
    per_shard = NIMG // (N_ORIENT * group_count)
    grouped_images = images.reshape(N_ORIENT, group_count, per_shard, 2 * K)
    grouped_offsets = offsets.reshape(N_ORIENT, group_count, per_shard, 2)
    half_norm = 0.5 * jnp.sum(jnp.square(slices.astype(jnp.float32)), axis=1)

    def one_group(carry, group_index):
        rows = lax.dynamic_index_in_dim(grouped_images, group_index, 1, keepdims=False).reshape(N_ORIENT * per_shard, 2 * K)
        shifts = lax.dynamic_index_in_dim(grouped_offsets, group_index, 1, keepdims=False).reshape(N_ORIENT * per_shard, 2)
        shifted = shift_images(rows, shifts)
        intersections = lax.dot_general(shifted, slices, (((1,), (1,)), ((), ())), preferred_element_type=jnp.float32)
        score = inv_noise * (intersections - half_norm[None, :])
        per_image = score.reshape(N_ORIENT * per_shard, SHIFTS * ORIENT)
        top_score = jnp.max(per_image, axis=1, keepdims=True)
        exp_terms = jnp.exp(per_image - top_score)
        mass_total = jnp.sum(exp_terms, axis=1, keepdims=True)
        posterior = (exp_terms / mass_total).astype(jnp.bfloat16).reshape(-1, ORIENT)
        partial_value = lax.dot_general(posterior, shifted, (((0,), (0,)), ((), ())), preferred_element_type=jnp.float32)
        part_mass = jnp.sum(posterior.astype(jnp.float32), axis=0)
        partial_value = lax.optimization_barrier(partial_value.astype(jnp.bfloat16)).astype(jnp.float32)
        part_mass = lax.optimization_barrier(part_mass.astype(jnp.bfloat16)).astype(jnp.float32)
        return (carry[0] + partial_value, carry[1] + part_mass), None

    start = (jnp.zeros((ORIENT, 2 * K), jnp.float32), jnp.zeros((ORIENT,), jnp.float32))
    (slice_sum, slice_mass), _ = lax.scan(one_group, start, jnp.arange(group_count, dtype=jnp.int32))

    segments = slice_sum.reshape(ORIENT, 2, NSEG, SEG).transpose(0, 2, 1, 3).reshape(ORIENT * NSEG, 2, SEG)
    seg_index = jnp.arange(ORIENT * NSEG, dtype=jnp.int32)
    target_key = seg_map[:, 0].astype(jnp.int32) * NSEG + seg_index % NSEG
    seg_total = jax.ops.segment_sum(segments, target_key, num_segments=NBRICK * NSEG).reshape(NBRICK, NSEG, 2, SEG)
    mass_rows = jnp.repeat(slice_mass, NSEG)
    mass_total = jax.ops.segment_sum(mass_rows, target_key, num_segments=NBRICK * NSEG).reshape(NBRICK, NSEG)

    def insert(packed):
        seg_block, mass_block, weight_block = packed
        weights = weight_block.astype(jnp.float32) * interp_scale
        values = jnp.einsum("jps,jsv->pv", seg_block, weights, precision=lax.Precision.HIGHEST)
        coverage = jnp.sum(weights, axis=1)
        weight_out = jnp.einsum("j,jv->v", mass_block, coverage, precision=lax.Precision.HIGHEST)
        return values, weight_out

    brick_values, brick_weight = lax.map(insert, (seg_total, mass_total, interp))
    return brick_values, brick_weight
```

```python
import functools
import numpy as np
import jax
import jax.numpy as jnp
from jax import lax
from jax.experimental import pallas as pl
from jax.experimental.pallas import tpu as pltpu
from jax.sharding import PartitionSpec as P

SHIFTS = 16
SEG = 256
LANES = 128
frame_side = 64
MESH = pl.DeviceIdType.MESH
f32 = jnp.float32
bf16 = jnp.bfloat16


def turn(index):
    index = index - frame_side * jnp.floor(index * (1.0 / frame_side) + 0.5)
    x = index * f32(np.pi / frame_side)
    y = x * x
    s = x * (1 + y * (-1 / 6 + y * (1 / 120 + y * (-1 / 5040 + y * (1 / 362880 + y * (-1 / 39916800 + y * (1 / 6227020800.0)))))))
    c = 1 + y * (-1 / 2 + y * (1 / 24 + y * (-1 / 720 + y * (1 / 40320 + y * (-1 / 3628800 + y * (1 / 479001600.0))))))
    return 1 - 2 * s * s, 2 * s * c


def nt(a, b):
    return lax.dot_general(a, b, (((1,), (1,)), ((), ())), preferred_element_type=f32)


def body(cfg, images, offs, slices_hbm, seg_t, interp_hbm, cos_tab, sin_tab, values_out, weight_out,
         img_buf, slices, interp, weights, shifted, terms, half_norm, hits, tops, stats, acc, mass_acc,
         msg, inbox, load_sem, send_r, send_l, recv_l, recv_r, stat_send, stat_recv, msg_send, msg_recv):
    n_or, n_img, n_brick, halves = cfg
    n_grp = n_img * n_brick
    n_dev = n_or * n_grp
    per, width = images.shape
    k_count = width // 2
    pp = per // halves
    rows = pp * SHIFTS
    together = max(1, 16 // pp)
    seg_count = k_count // SEG
    orients = slices.shape[0]
    inv_noise = 100.0 / k_count
    o = lax.axis_index("orient")
    group = lax.axis_index("img") * n_brick + lax.axis_index("brick")
    me = o * n_grp + group

    def place(flat):
        return {"orient": flat // n_grp, "img": (flat // n_brick) % n_img, "brick": flat % n_brick}

    load_slices = pltpu.make_async_copy(slices_hbm, slices, load_sem.at[0])
    load_interp = pltpu.make_async_copy(interp_hbm.at[0], interp, load_sem.at[1])
    load_slices.start()
    load_interp.start()

    barrier = pltpu.get_barrier_semaphore()

    def greet(i, c):
        pl.semaphore_signal(barrier, inc=1, device_id=place((me + i) % n_dev), device_id_type=MESH)
        return c

    lax.fori_loop(1, n_dev, greet, 0)
    pl.semaphore_wait(barrier, n_dev - 1)

    def part_of(ref, k, h):
        return ref.at[k, pl.ds(h * pp, pp), :]

    def to_right(t, h):
        k = jnp.maximum(o - t, 0)
        ref = part_of(img_buf, k, h)
        return pltpu.make_async_remote_copy(ref, ref, send_r.at[t, h], recv_l.at[t + 1, h],
                                            device_id={"orient": jnp.minimum(o + 1, n_or - 1)}, device_id_type=MESH)

    def to_left(t, h):
        k = jnp.minimum(o + t, n_or - 1)
        ref = part_of(img_buf, k, h)
        return pltpu.make_async_remote_copy(ref, ref, send_l.at[t, h], recv_r.at[t + 1, h],
                                            device_id={"orient": jnp.maximum(o - 1, 0)}, device_id_type=MESH)

    def from_left(t, h):
        ref = part_of(img_buf, jnp.maximum(o - t, 0), h)
        return pltpu.make_async_remote_copy(ref, ref, send_r.at[t, h], recv_l.at[t, h],
                                            device_id={"orient": jnp.maximum(o - 1, 0)}, device_id_type=MESH)

    def from_right(t, h):
        ref = part_of(img_buf, jnp.minimum(o + t, n_or - 1), h)
        return pltpu.make_async_remote_copy(ref, ref, send_l.at[t, h], recv_r.at[t, h],
                                            device_id={"orient": jnp.minimum(o + 1, n_or - 1)}, device_id_type=MESH)

    img_buf[o] = images[...]
    for h in range(halves):
        @pl.when(o < n_or - 1)
        def _():
            to_right(0, h).start()

        @pl.when(o > 0)
        def _():
            to_left(0, h).start()

    load_slices.wait()

    def squares(b, total):
        block = slices[:, pl.ds(pl.multiple_of(b * LANES, LANES), LANES)].astype(f32)
        return total + block * block

    norm = lax.fori_loop(0, width // LANES, squares, jnp.zeros((orients, LANES), f32))
    norm = 0.5 * jnp.sum(norm, axis=1, keepdims=True)
    diag = lax.broadcasted_iota(jnp.int32, (orients, orients), 0) == lax.broadcasted_iota(jnp.int32, (orients, orients), 1)
    half_norm[...] = jnp.sum(jnp.where(diag, norm, 0.0), axis=0, keepdims=True)

    seg = seg_t[...]

    def hit_rows(b, c):
        hits[b] = jnp.where(seg == b, 1.0, 0.0).astype(f32)
        return c

    lax.fori_loop(0, n_dev, hit_rows, 0)

    acc[...] = jnp.zeros_like(acc)
    mass_acc[...] = jnp.zeros_like(mass_acc)

    lane = lax.broadcasted_iota(jnp.int32, (pp, LANES), 1)
    freq = (lane % frame_side - frame_side // 2).astype(f32)
    odd = (lane // frame_side).astype(f32)
    same = lax.broadcasted_iota(jnp.int32, (pp, LANES), 0) == lane
    row8 = lax.broadcasted_iota(jnp.int32, (8, LANES), 0)
    per_block = LANES // frame_side

    def score(k, h):
        q = k * halves + h
        base = q * rows
        off = offs[pl.ds(pl.multiple_of((k * n_grp + group) * per + h * pp, 8), pp), :]
        a = (off[:, 0:1] - 2).astype(f32)
        b = (off[:, 1:2] - 2).astype(f32)
        start = turn(a * freq + b * odd)
        step_c, step_s = turn(jnp.broadcast_to(b * per_block, (pp, LANES)))

        def columns(kb, cs):
            ec, es = cs
            at_r = pl.ds(pl.multiple_of(kb * LANES, LANES), LANES)
            at_i = pl.ds(pl.multiple_of(k_count + kb * LANES, LANES), LANES)
            xr = img_buf[k, pl.ds(h * pp, pp), at_r].astype(f32)
            xi = img_buf[k, pl.ds(h * pp, pp), at_i].astype(f32)
            yr = xr * ec + xi * es
            yi = xi * ec - xr * es
            for s in range(0, SHIFTS, together):
                zr, zi = [], []
                for e in range(s, s + together):
                    c = cos_tab[e:e + 1, at_r]
                    d = sin_tab[e:e + 1, at_r]
                    zr.append(yr * c + yi * d)
                    zi.append(yi * c - yr * d)
                at = pl.ds(pl.multiple_of(base + s * pp, together * pp), together * pp)
                shifted[at, at_r] = jnp.concatenate(zr, axis=0).astype(bf16)
                shifted[at, at_i] = jnp.concatenate(zi, axis=0).astype(bf16)
            return ec * step_c - es * step_s, es * step_c + ec * step_s

        lax.fori_loop(0, k_count // LANES, columns, start)
        at = pl.ds(pl.multiple_of(base, rows), rows)
        got = inv_noise * (nt(shifted[at, :], slices[...]) - half_norm[...])
        got = got.reshape(SHIFTS, pp, orients)
        top = jnp.max(jnp.max(got, axis=0), axis=1, keepdims=True)
        term = jnp.exp(got - top[None])
        mass = jnp.sum(jnp.sum(term, axis=0), axis=1, keepdims=True)
        terms[at, :] = term.reshape(rows, orients)
        tops[q] = jnp.broadcast_to(top, (pp, LANES))
        top_row = jnp.sum(jnp.where(same, top, 0.0), axis=0, keepdims=True)
        mass_row = jnp.sum(jnp.where(same, mass, 0.0), axis=0, keepdims=True)
        stats[q, 0] = jnp.where(row8 == 0, top_row, mass_row)
        for i in range(1, n_or):
            stat_copy(q, i).start()

    def stat_copy(q, i):
        return pltpu.make_async_remote_copy(stats.at[q, 0], stats.at[q, i], stat_send.at[q, i], stat_recv.at[q, i],
                                            device_id={"orient": (o + i) % n_or}, device_id_type=MESH)

    def distance(step, c):
        t, h = step // halves, step % halves
        has_left = (t > 0) & (o - t >= 0)
        has_right = (t > 0) & (o + t < n_or)

        @pl.when(has_left)
        def _():
            from_left(t, h).wait_recv()

        @pl.when(has_left & (o < n_or - 1))
        def _():
            to_right(t, h).start()

        @pl.when(has_right)
        def _():
            from_right(t, h).wait_recv()

        @pl.when(has_right & (o > 0))
        def _():
            to_left(t, h).start()

        def side(d, c):
            k = o + t * (2 * d - 1)
            live = (k >= 0) & (k < n_or) & ((t > 0) | (d == 0))

            @pl.when(live)
            def _():
                score(k, h)
            return c

        return lax.fori_loop(0, 2, side, c)

    lax.fori_loop(0, n_or * halves, distance, 0)

    load_interp.wait()

    def split(j, c):
        w = interp[j]
        weights[j, :, 0:SEG] = (w >> 4).astype(f32).astype(bf16)
        weights[j, :, SEG:2 * SEG] = (w & 15).astype(f32).astype(bf16)
        return c

    lax.fori_loop(0, seg_count, split, 0)

    hit = hits[...].reshape(n_dev * seg_count, orients).astype(bf16)
    seg_row = lax.broadcasted_iota(jnp.int32, (n_dev * seg_count, SEG), 0) % seg_count

    def collect(step, c):
        m, h = step // halves, step % halves
        if n_or % 2 == 0:
            k = n_or // 2 + (m % 2) * (m // 2) - (1 - m % 2) * (m // 2 + 1)
        else:
            k = m
        q = k * halves + h

        def arrive(i, c):
            stat_copy(q, i).wait_recv()
            return c

        lax.fori_loop(1, n_or, arrive, 0)
        every = [stats[q, i] for i in range(n_or)]
        top = functools.reduce(jnp.maximum, [e[0:1] for e in every])
        mass = functools.reduce(jnp.add, [e[1:2] * jnp.exp(e[0:1] - top) for e in every])
        top = jnp.sum(jnp.where(same, top, 0.0), axis=1, keepdims=True)
        mass = jnp.sum(jnp.where(same, mass, 0.0), axis=1, keepdims=True)
        factor = jnp.exp(tops[q][:, 0:1] - top) / mass
        at = pl.ds(pl.multiple_of(q * rows, rows), rows)
        post = terms[at, :].reshape(SHIFTS, pp, orients) * factor[None]
        post = post.reshape(rows, orients).astype(bf16)
        share = nt(hit, post)
        mass_acc[...] += jnp.broadcast_to(jnp.sum(share, axis=1, keepdims=True), mass_acc.shape)
        share = share.astype(bf16)
        for p in range(2):
            total = acc[p]
            for j in range(seg_count):
                c0 = p * k_count + j * SEG
                got = jnp.dot(share, shifted[at, c0:c0 + SEG], preferred_element_type=f32)
                total = jnp.where(seg_row == j, total + got, total)
            acc[p] = total
        return c

    lax.fori_loop(0, n_or * halves, collect, 0)

    def pack(b, c):
        at = pl.ds(pl.multiple_of(b * seg_count, seg_count), seg_count)
        msg[b, :, 0:SEG] = jnp.concatenate([acc[0, at, :], acc[1, at, :]], axis=0).astype(bf16)
        m = mass_acc[at, :]
        hi = m.astype(bf16).astype(f32)
        msg[b, :, SEG:SEG + LANES] = jnp.concatenate([hi, m - hi], axis=0).astype(bf16)
        return c

    lax.fori_loop(0, n_dev, pack, 0)

    def msg_copy(i):
        to = (me + i) % n_dev
        return pltpu.make_async_remote_copy(msg.at[to], inbox.at[i], msg_send.at[i], msg_recv.at[i],
                                            device_id=place(to), device_id_type=MESH)

    def post_msg(i, c):
        msg_copy(i).start()
        return c

    lax.fori_loop(1, n_dev, post_msg, 0)

    def take(i, total):
        msg_copy(i).wait_recv()
        return total + inbox[i].astype(f32)

    total = lax.fori_loop(1, n_dev, take, msg[me].astype(f32))
    mass = total[0:seg_count, SEG:] + total[seg_count:, SEG:]
    left = jnp.concatenate([total[:, 0:SEG], jnp.concatenate([mass, mass], axis=1)], axis=0)
    n_rows = 3 * seg_count
    hi = left.astype(bf16).astype(f32)
    both = jnp.concatenate([hi, left - hi], axis=0).astype(bf16)
    place_row = lax.broadcasted_iota(jnp.int32, (n_rows, SEG), 0) % seg_count
    result = jnp.zeros((n_rows, SEG), f32)
    for j in range(seg_count):
        got = jnp.dot(both, weights[j], preferred_element_type=f32)
        got = got[0:n_rows] + got[n_rows:]
        got = got[:, 0:SEG] * (16.0 / 256.0) + got[:, SEG:] * (1.0 / 256.0)
        result = jnp.where(place_row == j, got, result)
    result = jnp.sum(result.reshape(3, seg_count, SEG), axis=1)
    values_out[...] = result[0:2]
    weight_out[...] = result[2:3]

    def settle(step, c):
        t, h = step // halves, step % halves

        @pl.when((o < n_or - 1) & (o - t >= 0))
        def _():
            to_right(t, h).wait_send()

        @pl.when((o > 0) & (o + t < n_or))
        def _():
            to_left(t, h).wait_send()
        return c

    lax.fori_loop(0, (n_or - 1) * halves, settle, 0)

    def settle_stats(q, c):
        for i in range(1, n_or):
            stat_copy(q, i).wait_send()
        return c

    lax.fori_loop(0, n_or * halves, settle_stats, 0)

    def settle_msgs(i, c):
        msg_copy(i).wait_send()
        return c

    lax.fori_loop(1, n_dev, settle_msgs, 0)


def per_device(images, offsets, slices, seg_map, interp):
    n_or = lax.axis_size("orient")
    n_img = lax.axis_size("img")
    n_brick = lax.axis_size("brick")
    n_dev = n_or * n_img * n_brick
    per, width = images.shape
    k_count = width // 2
    seg_count = k_count // SEG
    orients = slices.shape[0]
    halves = 2 if per % 32 == 0 else 1
    pp = per // halves
    rows = pp * SHIFTS
    pieces = n_or * halves
    coef = np.arange(k_count)
    shift = np.arange(SHIFTS)
    index = ((shift % 4)[:, None] * (coef % frame_side - frame_side // 2)[None, :]
             + (shift // 4)[:, None] * (coef // frame_side)[None, :]) % frame_side
    angle = 2 * np.pi * index / frame_side
    cos_tab = jnp.asarray(np.cos(angle), f32)
    sin_tab = jnp.asarray(np.sin(angle), f32)
    own_seg = lax.dynamic_index_in_dim(
        seg_map.reshape(n_or, orients, seg_count), lax.axis_index("orient"), 0, keepdims=False).T
    vmem = pl.BlockSpec(memory_space=pltpu.VMEM)
    hbm = pl.BlockSpec(memory_space=pl.ANY)
    dma = pltpu.SemaphoreType.DMA
    values, weight = pl.pallas_call(
        functools.partial(body, (n_or, n_img, n_brick, halves)),
        out_shape=(jax.ShapeDtypeStruct((2, SEG), f32), jax.ShapeDtypeStruct((1, SEG), f32)),
        in_specs=[vmem, vmem, hbm, vmem, hbm, vmem, vmem],
        out_specs=(vmem, vmem),
        scratch_shapes=[
            pltpu.VMEM((n_or, per, width), bf16),
            pltpu.VMEM((orients, width), bf16),
            pltpu.VMEM((seg_count, SEG, SEG), jnp.int32),
            pltpu.VMEM((seg_count, SEG, 2 * SEG), bf16),
            pltpu.VMEM((pieces * rows, width), bf16),
            pltpu.VMEM((pieces * rows, orients), f32),
            pltpu.VMEM((1, orients), f32),
            pltpu.VMEM((n_dev, seg_count, orients), f32),
            pltpu.VMEM((pieces, pp, LANES), f32),
            pltpu.VMEM((pieces, n_or, 8, LANES), f32),
            pltpu.VMEM((2, n_dev * seg_count, SEG), f32),
            pltpu.VMEM((n_dev * seg_count, LANES), f32),
            pltpu.VMEM((n_dev, 2 * seg_count, SEG + LANES), bf16),
            pltpu.VMEM((n_dev, 2 * seg_count, SEG + LANES), bf16),
            dma((2,)),
            dma((n_or, halves)),
            dma((n_or, halves)),
            dma((n_or + 1, halves)),
            dma((n_or + 1, halves)),
            dma((pieces, n_or)),
            dma((pieces, n_or)),
            dma((n_dev,)),
            dma((n_dev,)),
        ],
        compiler_params=pltpu.CompilerParams(
            collective_id=0, has_side_effects=True, vmem_limit_bytes=56 * 1024 * 1024),
        name="score_and_insert",
    )(images, offsets, slices, own_seg, interp, cos_tab, sin_tab)
    return values[None], weight


def solution(mesh):
    placed = (
        P(("groups", "orient", "img", "brick"), None),
        P("groups", None),
        P(("groups", "orient"), None),
        P(),
        P(("orient", "img", "brick"), None, None, None),
    )
    return jax.shard_map(
        per_device,
        mesh=mesh,
        in_specs=placed,
        out_specs=(
            P(("groups", "orient", "img", "brick"), None, None),
            P(("groups", "orient", "img", "brick"), None),
        ),
        check_vma=False,
    )
```

```python
import functools
import numpy as np
import jax
import jax.numpy as jnp
from jax import lax
from jax.experimental import pallas as pl
from jax.experimental.pallas import tpu as pltpu
from jax.sharding import PartitionSpec as P

SHIFTS = 16
SEG = 256
LANES = 128
frame_side = 64
MESH = pl.DeviceIdType.MESH
f32 = jnp.float32
bf16 = jnp.bfloat16


def turn(index):
    index = index - frame_side * jnp.floor(index * (1.0 / frame_side) + 0.5)
    x = index * f32(np.pi / frame_side)
    y = x * x
    s = x * (1 + y * (-1 / 6 + y * (1 / 120 + y * (-1 / 5040 + y * (1 / 362880 + y * (-1 / 39916800 + y * (1 / 6227020800.0)))))))
    c = 1 + y * (-1 / 2 + y * (1 / 24 + y * (-1 / 720 + y * (1 / 40320 + y * (-1 / 3628800 + y * (1 / 479001600.0))))))
    return 1 - 2 * s * s, 2 * s * c


def nt(a, b):
    return lax.dot_general(a, b, (((1,), (1,)), ((), ())), preferred_element_type=f32)


def body(cfg, images, offs, slices_hbm, seg_map, interp_hbm, cos_tab, sin_tab, result_out,
         img_buf, slices, interp, weights, shifted, terms, half_norm, hits, tops, stats, shares, off_a, off_b, acc, mass_acc,
         msg, inbox, load_sem, send_r, send_l, recv_l, recv_r, stat_send, stat_recv, msg_send, msg_recv):
    n_or, n_img, n_brick, halves = cfg
    n_grp = n_img * n_brick
    n_dev = n_or * n_grp
    per, width = images.shape
    k_count = width // 2
    pp = per // halves
    rows = pp * SHIFTS
    together = max(1, 16 // pp)
    seg_count = k_count // SEG
    orients = slices.shape[0]
    inv_noise = 100.0 / k_count
    o = lax.axis_index("orient")
    group = lax.axis_index("img") * n_brick + lax.axis_index("brick")
    me = o * n_grp + group

    def place(flat):
        return {"orient": flat // n_grp, "img": (flat // n_brick) % n_img, "brick": flat % n_brick}

    load_slices = pltpu.make_async_copy(slices_hbm, slices, load_sem.at[0])
    load_interp = pltpu.make_async_copy(interp_hbm.at[0], interp, load_sem.at[1])
    load_slices.start()
    load_interp.start()

    barrier = pltpu.get_barrier_semaphore()

    def greet(i, c):
        pl.semaphore_signal(barrier, inc=1, device_id=place((me + i) % n_dev), device_id_type=MESH)
        return c

    lax.fori_loop(1, n_dev, greet, 0)
    pl.semaphore_wait(barrier, n_dev - 1)

    def part_of(ref, k, h):
        return ref.at[k, pl.ds(h * pp, pp), :]

    def to_right(t, h):
        k = jnp.maximum(o - t, 0)
        ref = part_of(img_buf, k, h)
        return pltpu.make_async_remote_copy(ref, ref, send_r.at[t, h], recv_l.at[t + 1, h],
                                            device_id={"orient": jnp.minimum(o + 1, n_or - 1)}, device_id_type=MESH)

    def to_left(t, h):
        k = jnp.minimum(o + t, n_or - 1)
        ref = part_of(img_buf, k, h)
        return pltpu.make_async_remote_copy(ref, ref, send_l.at[t, h], recv_r.at[t + 1, h],
                                            device_id={"orient": jnp.maximum(o - 1, 0)}, device_id_type=MESH)

    def from_left(t, h):
        ref = part_of(img_buf, jnp.maximum(o - t, 0), h)
        return pltpu.make_async_remote_copy(ref, ref, send_r.at[t, h], recv_l.at[t, h],
                                            device_id={"orient": jnp.maximum(o - 1, 0)}, device_id_type=MESH)

    def from_right(t, h):
        ref = part_of(img_buf, jnp.minimum(o + t, n_or - 1), h)
        return pltpu.make_async_remote_copy(ref, ref, send_l.at[t, h], recv_r.at[t, h],
                                            device_id={"orient": jnp.minimum(o + 1, n_or - 1)}, device_id_type=MESH)

    img_buf[o] = images[...]
    for h in range(halves):
        @pl.when(o < n_or - 1)
        def _():
            to_right(0, h).start()

        @pl.when(o > 0)
        def _():
            to_left(0, h).start()

    load_slices.wait()

    def squares(b, total):
        block = slices[:, pl.ds(pl.multiple_of(b * LANES, LANES), LANES)].astype(f32)
        return total + block * block

    norm = lax.fori_loop(0, width // LANES, squares, jnp.zeros((orients, LANES), f32))
    norm = 0.5 * jnp.sum(norm, axis=1, keepdims=True)
    diag = lax.broadcasted_iota(jnp.int32, (orients, orients), 0) == lax.broadcasted_iota(jnp.int32, (orients, orients), 1)
    half_norm[...] = jnp.sum(jnp.where(diag, norm, 0.0), axis=0, keepdims=True)

    span = SEG // seg_count
    seg_lane = lax.broadcasted_iota(jnp.int32, (seg_count, SEG), 1) % seg_count
    own_j = seg_lane == lax.broadcasted_iota(jnp.int32, (seg_count, SEG), 0)
    src = lax.broadcasted_iota(jnp.int32, (SEG, orients), 0) // seg_count
    dst = lax.broadcasted_iota(jnp.int32, (SEG, orients), 1)

    def regroup(t, total):
        at = pl.ds(pl.multiple_of((o * orients + t * span) * seg_count, SEG), SEG)
        ids = jnp.where(own_j, seg_map[:, at].astype(f32), 0.0).astype(bf16)
        to = jnp.where(src + t * span == dst, 1.0, 0.0).astype(bf16)
        return total + jnp.dot(ids, to, preferred_element_type=f32)

    seg = lax.fori_loop(0, orients // span, regroup, jnp.zeros((seg_count, orients), f32)).astype(jnp.int32)

    image_rows = n_or * per
    picked = lax.broadcasted_iota(jnp.int32, (image_rows, image_rows * n_grp), 0)
    picked = ((picked // per) * n_grp + group) * per + picked % per
    picked = picked == lax.broadcasted_iota(jnp.int32, (image_rows, image_rows * n_grp), 1)
    off = (offs[...] - 2).astype(f32)
    for ref, row in ((off_a, off[0:1]), (off_b, off[1:2])):
        ref[...] = jnp.broadcast_to(jnp.sum(jnp.where(picked, row, 0.0), axis=1, keepdims=True), (image_rows, LANES))

    def hit_rows(b, c):
        hits[b] = jnp.where(seg == b, 1.0, 0.0).astype(f32)
        return c

    lax.fori_loop(0, n_dev, hit_rows, 0)

    mass_acc[...] = jnp.zeros_like(mass_acc)

    lane = lax.broadcasted_iota(jnp.int32, (pp, LANES), 1)
    freq = (lane % frame_side - frame_side // 2).astype(f32)
    odd = (lane // frame_side).astype(f32)
    same = lax.broadcasted_iota(jnp.int32, (pp, LANES), 0) == lane
    row8 = lax.broadcasted_iota(jnp.int32, (8, LANES), 0)
    per_block = LANES // frame_side

    def score(k, h):
        q = k * halves + h
        base = q * rows
        at_image = pl.ds(pl.multiple_of(k * per + h * pp, 8), pp)
        a = off_a[at_image, :]
        b = off_b[at_image, :]
        start = turn(a * freq + b * odd)
        step_c, step_s = turn(b * per_block)

        def columns(kb, cs):
            ec, es = cs
            at_r = pl.ds(pl.multiple_of(kb * LANES, LANES), LANES)
            at_i = pl.ds(pl.multiple_of(k_count + kb * LANES, LANES), LANES)
            xr = img_buf[k, pl.ds(h * pp, pp), at_r].astype(f32)
            xi = img_buf[k, pl.ds(h * pp, pp), at_i].astype(f32)
            yr = xr * ec + xi * es
            yi = xi * ec - xr * es
            for s in range(0, SHIFTS, together):
                zr, zi = [], []
                for e in range(s, s + together):
                    c = cos_tab[e:e + 1, at_r]
                    d = sin_tab[e:e + 1, at_r]
                    zr.append(yr * c + yi * d)
                    zi.append(yi * c - yr * d)
                at = pl.ds(pl.multiple_of(base + s * pp, together * pp), together * pp)
                shifted[at, at_r] = jnp.concatenate(zr, axis=0).astype(bf16)
                shifted[at, at_i] = jnp.concatenate(zi, axis=0).astype(bf16)
            return ec * step_c - es * step_s, es * step_c + ec * step_s

        lax.fori_loop(0, k_count // LANES, columns, start)
        at = pl.ds(pl.multiple_of(base, rows), rows)
        got = inv_noise * (nt(shifted[at, :], slices[...]) - half_norm[...])
        got = got.reshape(SHIFTS, pp, orients)
        top = jnp.max(jnp.max(got, axis=0), axis=1, keepdims=True)
        term = jnp.exp(got - top[None])
        mass = jnp.sum(jnp.sum(term, axis=0), axis=1, keepdims=True)
        terms[at, :] = term.reshape(rows, orients)
        tops[q] = jnp.broadcast_to(top, (pp, LANES))
        top_row = jnp.sum(jnp.where(same, top, 0.0), axis=0, keepdims=True)
        mass_row = jnp.sum(jnp.where(same, mass, 0.0), axis=0, keepdims=True)
        stats[q, 0] = jnp.where(row8 == 0, top_row, mass_row)
        for i in range(1, n_or):
            stat_copy(q, i).start()

    def stat_copy(q, i):
        return pltpu.make_async_remote_copy(stats.at[q, 0], stats.at[q, i], stat_send.at[q, i], stat_recv.at[q, i],
                                            device_id={"orient": (o + i) % n_or}, device_id_type=MESH)

    def distance(step, c):
        t, h = step // halves, step % halves
        has_left = (t > 0) & (o - t >= 0)
        has_right = (t > 0) & (o + t < n_or)

        @pl.when(has_left)
        def _():
            from_left(t, h).wait_recv()

        @pl.when(has_left & (o < n_or - 1))
        def _():
            to_right(t, h).start()

        @pl.when(has_right)
        def _():
            from_right(t, h).wait_recv()

        @pl.when(has_right & (o > 0))
        def _():
            to_left(t, h).start()

        def side(d, c):
            k = o + t * (2 * d - 1)
            live = (k >= 0) & (k < n_or) & ((t > 0) | (d == 0))

            @pl.when(live)
            def _():
                score(k, h)
            return c

        return lax.fori_loop(0, 2, side, c)

    hit_all = hits.reshape(n_dev * seg_count, orients)
    seg_row = lax.broadcasted_iota(jnp.int32, (n_dev * seg_count, SEG), 0) % seg_count

    def collect(step, c):
        k, h = c + step // halves, step % halves
        q = k * halves + h

        def arrive(i, c):
            stat_copy(q, i).wait_recv()
            return c

        lax.fori_loop(1, n_or, arrive, 0)
        every = [stats[q, i] for i in range(n_or)]
        top = functools.reduce(jnp.maximum, [e[0:1] for e in every])
        mass = functools.reduce(jnp.add, [e[1:2] * jnp.exp(e[0:1] - top) for e in every])
        top = jnp.sum(jnp.where(same, top, 0.0), axis=1, keepdims=True)
        mass = jnp.sum(jnp.where(same, mass, 0.0), axis=1, keepdims=True)
        factor = jnp.exp(tops[q][:, 0:1] - top) / mass
        at = pl.ds(pl.multiple_of(q * rows, rows), rows)
        post = terms[at, :].reshape(SHIFTS, pp, orients) * factor[None]
        post = post.reshape(rows, orients).astype(bf16)
        share = nt(hit_all[...].astype(bf16), post)
        mass_acc[...] += jnp.broadcast_to(jnp.sum(share, axis=1, keepdims=True), mass_acc.shape)
        shares[:, at] = share.astype(bf16)
        return c

    def gather_in(first, last, fresh):
        lax.fori_loop(0, (last - first) * halves, collect, first)
        lo, hi = first * halves * rows, last * halves * rows
        for p in range(2):
            total = None if fresh else acc[p]
            for j in range(seg_count):
                c0 = p * k_count + j * SEG
                got = jnp.dot(shares[:, lo:hi], shifted[lo:hi, c0:c0 + SEG], preferred_element_type=f32)
                if fresh:
                    total = got if total is None else jnp.where(seg_row == j, got, total)
                else:
                    total = jnp.where(seg_row == j, total + got, total)
            acc[p] = total

    quarter = n_or // 4
    steps = n_or * halves
    early = (n_or - 1) * halves if quarter else steps
    lax.fori_loop(0, early, distance, 0)
    if quarter:
        gather_in(quarter, n_or - quarter, True)
        lax.fori_loop(early, steps, distance, 0)

    load_interp.wait()

    def split(j, c):
        w = interp[j]
        weights[j, :, 0:SEG] = (w >> 4).astype(f32).astype(bf16)
        weights[j, :, SEG:2 * SEG] = (w & 15).astype(f32).astype(bf16)
        return c

    lax.fori_loop(0, seg_count, split, 0)

    if quarter:
        gather_in(0, quarter, False)
        gather_in(n_or - quarter, n_or, False)
    else:
        gather_in(0, n_or, True)

    def pack(b, c):
        at = pl.ds(pl.multiple_of(b * seg_count, seg_count), seg_count)
        msg[b, :, 0:SEG] = jnp.concatenate([acc[0, at, :], acc[1, at, :]], axis=0).astype(bf16)
        m = mass_acc[at, :]
        hi = m.astype(bf16).astype(f32)
        msg[b, :, SEG:SEG + LANES] = jnp.concatenate([hi, m - hi], axis=0).astype(bf16)
        return c

    lax.fori_loop(0, n_dev, pack, 0)

    def msg_copy(i):
        to = (me + i) % n_dev
        return pltpu.make_async_remote_copy(msg.at[to], inbox.at[i], msg_send.at[i], msg_recv.at[i],
                                            device_id=place(to), device_id_type=MESH)

    def post_msg(i, c):
        msg_copy(i).start()
        return c

    lax.fori_loop(1, n_dev, post_msg, 0)

    def take(i, total):
        msg_copy(i).wait_recv()
        return total + inbox[i].astype(f32)

    total = lax.fori_loop(1, n_dev, take, msg[me].astype(f32))
    mass = total[0:seg_count, SEG:] + total[seg_count:, SEG:]
    left = jnp.concatenate([total[:, 0:SEG], jnp.concatenate([mass, mass], axis=1)], axis=0)
    n_rows = 3 * seg_count
    hi = left.astype(bf16).astype(f32)
    both = jnp.concatenate([hi, left - hi], axis=0).astype(bf16)
    place_row = lax.broadcasted_iota(jnp.int32, (n_rows, SEG), 0) % seg_count
    result = jnp.zeros((n_rows, SEG), f32)
    for j in range(seg_count):
        got = jnp.dot(both, weights[j], preferred_element_type=f32)
        got = got[0:n_rows] + got[n_rows:]
        got = got[:, 0:SEG] * (16.0 / 256.0) + got[:, SEG:] * (1.0 / 256.0)
        result = jnp.where(place_row == j, got, result)
    result = jnp.sum(result.reshape(3, seg_count, SEG), axis=1)
    result_out[...] = result

    def settle(step, c):
        t, h = step // halves, step % halves

        @pl.when((o < n_or - 1) & (o - t >= 0))
        def _():
            to_right(t, h).wait_send()

        @pl.when((o > 0) & (o + t < n_or))
        def _():
            to_left(t, h).wait_send()
        return c

    lax.fori_loop(0, (n_or - 1) * halves, settle, 0)

    def settle_stats(q, c):
        for i in range(1, n_or):
            stat_copy(q, i).wait_send()
        return c

    lax.fori_loop(0, n_or * halves, settle_stats, 0)

    def settle_msgs(i, c):
        msg_copy(i).wait_send()
        return c

    lax.fori_loop(1, n_dev, settle_msgs, 0)


def hand_out(result, values_out, weight_out):
    values_out[0] = result[0:2]
    weight_out[...] = result[2:3]


def per_device(images, offsets, slices, seg_map, interp):
    n_or = lax.axis_size("orient")
    n_img = lax.axis_size("img")
    n_brick = lax.axis_size("brick")
    n_dev = n_or * n_img * n_brick
    per, width = images.shape
    k_count = width // 2
    seg_count = k_count // SEG
    orients = slices.shape[0]
    halves = 2 if per % 32 == 0 else 1
    pp = per // halves
    rows = pp * SHIFTS
    pieces = n_or * halves
    coef = np.arange(k_count)
    shift = np.arange(SHIFTS)
    index = ((shift % 4)[:, None] * (coef % frame_side - frame_side // 2)[None, :]
             + (shift // 4)[:, None] * (coef // frame_side)[None, :]) % frame_side
    angle = 2 * np.pi * index / frame_side
    cos_tab = jnp.asarray(np.cos(angle), f32)
    sin_tab = jnp.asarray(np.sin(angle), f32)
    vmem = pl.BlockSpec(memory_space=pltpu.VMEM)
    hbm = pl.BlockSpec(memory_space=pl.ANY)
    dma = pltpu.SemaphoreType.DMA
    result = pl.pallas_call(
        functools.partial(body, (n_or, n_img, n_brick, halves)),
        out_shape=jax.ShapeDtypeStruct((3, SEG), f32),
        in_specs=[vmem, vmem, hbm, vmem, hbm, vmem, vmem],
        out_specs=vmem,
        scratch_shapes=[
            pltpu.VMEM((n_or, per, width), bf16),
            pltpu.VMEM((orients, width), bf16),
            pltpu.VMEM((seg_count, SEG, SEG), jnp.int32),
            pltpu.VMEM((seg_count, SEG, 2 * SEG), bf16),
            pltpu.VMEM((pieces * rows, width), bf16),
            pltpu.VMEM((pieces * rows, orients), f32),
            pltpu.VMEM((1, orients), f32),
            pltpu.VMEM((n_dev, seg_count, orients), f32),
            pltpu.VMEM((pieces, pp, LANES), f32),
            pltpu.VMEM((pieces, n_or, 8, LANES), f32),
            pltpu.VMEM((n_dev * seg_count, pieces * rows), bf16),
            pltpu.VMEM((n_or * per, LANES), f32),
            pltpu.VMEM((n_or * per, LANES), f32),
            pltpu.VMEM((2, n_dev * seg_count, SEG), f32),
            pltpu.VMEM((n_dev * seg_count, LANES), f32),
            pltpu.VMEM((n_dev, 2 * seg_count, SEG + LANES), bf16),
            pltpu.VMEM((n_dev, 2 * seg_count, SEG + LANES), bf16),
            dma((2,)),
            dma((n_or, halves)),
            dma((n_or, halves)),
            dma((n_or + 1, halves)),
            dma((n_or + 1, halves)),
            dma((pieces, n_or)),
            dma((pieces, n_or)),
            dma((n_dev,)),
            dma((n_dev,)),
        ],
        compiler_params=pltpu.CompilerParams(
            collective_id=0, has_side_effects=True, vmem_limit_bytes=56 * 1024 * 1024),
        name="score_and_insert",
    )(images, offsets.T, slices, seg_map.T, interp, cos_tab, sin_tab)
    return pl.pallas_call(
        hand_out,
        out_shape=(jax.ShapeDtypeStruct((1, 2, SEG), f32), jax.ShapeDtypeStruct((1, SEG), f32)),
        in_specs=[vmem],
        out_specs=(vmem, vmem),
        name="hand_out",
    )(result)


def solution(mesh):
    placed = (
        P(("groups", "orient", "img", "brick"), None),
        P("groups", None),
        P(("groups", "orient"), None),
        P(),
        P(("orient", "img", "brick"), None, None, None),
    )
    return jax.shard_map(
        per_device,
        mesh=mesh,
        in_specs=placed,
        out_specs=(
            P(("groups", "orient", "img", "brick"), None, None),
            P(("groups", "orient", "img", "brick"), None),
        ),
        check_vma=False,
    )
```

```python
import functools
import numpy as np
import jax
import jax.numpy as jnp
from jax import lax
from jax.experimental import pallas as pl
from jax.experimental.pallas import tpu as pltpu
from jax.sharding import PartitionSpec as P

SHIFTS = 16
SEG = 256
LANES = 128
frame_side = 64
MESH = pl.DeviceIdType.MESH
f32 = jnp.float32
bf16 = jnp.bfloat16


def turn(index):
    index = index - frame_side * jnp.floor(index * (1.0 / frame_side) + 0.5)
    x = index * f32(np.pi / frame_side)
    y = x * x
    s = x * (1 + y * (-1 / 6 + y * (1 / 120 + y * (-1 / 5040 + y * (1 / 362880 + y * (-1 / 39916800 + y * (1 / 6227020800.0)))))))
    c = 1 + y * (-1 / 2 + y * (1 / 24 + y * (-1 / 720 + y * (1 / 40320 + y * (-1 / 3628800 + y * (1 / 479001600.0))))))
    return 1 - 2 * s * s, 2 * s * c


def nt(a, b):
    return lax.dot_general(a, b, (((1,), (1,)), ((), ())), preferred_element_type=f32)


def body(cfg, images, offs, slices_hbm, seg_map, interp_hbm, cos_tab, sin_tab, result_out,
         img_buf, slices, interp, weights, shifted, terms, half_norm, hits, tops, stats, shares, off_a, off_b, acc, by_brick, mass_acc,
         msg, inbox, load_sem, send_r, send_l, recv_l, recv_r, stat_send, stat_recv, msg_send, msg_recv):
    n_or, n_img, n_brick, halves = cfg
    n_grp = n_img * n_brick
    n_dev = n_or * n_grp
    per, width = images.shape
    k_count = width // 2
    pp = per // halves
    rows = pp * SHIFTS
    together = max(1, 16 // pp)
    seg_count = k_count // SEG
    orients = slices.shape[0]
    inv_noise = 100.0 / k_count
    o = lax.axis_index("orient")
    group = lax.axis_index("img") * n_brick + lax.axis_index("brick")
    me = o * n_grp + group

    def place(flat):
        return {"orient": flat // n_grp, "img": (flat // n_brick) % n_img, "brick": flat % n_brick}

    load_slices = pltpu.make_async_copy(slices_hbm, slices, load_sem.at[0])
    load_interp = pltpu.make_async_copy(interp_hbm.at[0], interp, load_sem.at[1])
    load_slices.start()
    load_interp.start()

    barrier = pltpu.get_barrier_semaphore()

    def greet(i, c):
        pl.semaphore_signal(barrier, inc=1, device_id=place((me + i) % n_dev), device_id_type=MESH)
        return c

    lax.fori_loop(1, n_dev, greet, 0)

    span = SEG // seg_count
    seg_lane = lax.broadcasted_iota(jnp.int32, (seg_count, SEG), 1) % seg_count
    own_j = seg_lane == lax.broadcasted_iota(jnp.int32, (seg_count, SEG), 0)
    src = lax.broadcasted_iota(jnp.int32, (SEG, orients), 0) // seg_count
    dst = lax.broadcasted_iota(jnp.int32, (SEG, orients), 1)

    def regroup(t, total):
        at = pl.ds(pl.multiple_of((o * orients + t * span) * seg_count, SEG), SEG)
        ids = jnp.where(own_j, seg_map[:, at].astype(f32), 0.0).astype(bf16)
        to = jnp.where(src + t * span == dst, 1.0, 0.0).astype(bf16)
        return total + jnp.dot(ids, to, preferred_element_type=f32)

    seg = lax.fori_loop(0, orients // span, regroup, jnp.zeros((seg_count, orients), f32)).astype(jnp.int32)

    image_rows = n_or * per
    picked = lax.broadcasted_iota(jnp.int32, (image_rows, image_rows * n_grp), 0)
    picked = ((picked // per) * n_grp + group) * per + picked % per
    picked = picked == lax.broadcasted_iota(jnp.int32, (image_rows, image_rows * n_grp), 1)
    off = offs[...].astype(f32) - 0.5
    for ref, row in ((off_a, off[0:1]), (off_b, off[1:2])):
        ref[...] = jnp.broadcast_to(jnp.sum(jnp.where(picked, row, 0.0), axis=1, keepdims=True), (image_rows, LANES))

    brick = lax.broadcasted_iota(jnp.int32, (n_dev, orients), 0)
    for j in range(seg_count):
        hits[j] = jnp.where(seg[j:j + 1] == brick, 1.0, 0.0).astype(bf16)

    img_buf[o] = images[...]
    pl.semaphore_wait(barrier, n_dev - 1)

    def part_of(ref, k, h):
        return ref.at[k, pl.ds(h * pp, pp), :]

    def to_right(t, h):
        k = jnp.maximum(o - t, 0)
        ref = part_of(img_buf, k, h)
        return pltpu.make_async_remote_copy(ref, ref, send_r.at[t, h], recv_l.at[t + 1, h],
                                            device_id={"orient": jnp.minimum(o + 1, n_or - 1)}, device_id_type=MESH)

    def to_left(t, h):
        k = jnp.minimum(o + t, n_or - 1)
        ref = part_of(img_buf, k, h)
        return pltpu.make_async_remote_copy(ref, ref, send_l.at[t, h], recv_r.at[t + 1, h],
                                            device_id={"orient": jnp.maximum(o - 1, 0)}, device_id_type=MESH)

    def from_left(t, h):
        ref = part_of(img_buf, jnp.maximum(o - t, 0), h)
        return pltpu.make_async_remote_copy(ref, ref, send_r.at[t, h], recv_l.at[t, h],
                                            device_id={"orient": jnp.maximum(o - 1, 0)}, device_id_type=MESH)

    def from_right(t, h):
        ref = part_of(img_buf, jnp.minimum(o + t, n_or - 1), h)
        return pltpu.make_async_remote_copy(ref, ref, send_l.at[t, h], recv_r.at[t, h],
                                            device_id={"orient": jnp.minimum(o + 1, n_or - 1)}, device_id_type=MESH)

    for h in range(halves):
        @pl.when(o < n_or - 1)
        def _():
            to_right(0, h).start()

        @pl.when(o > 0)
        def _():
            to_left(0, h).start()

    load_slices.wait()

    def squares(b, total):
        block = slices[:, pl.ds(pl.multiple_of(b * LANES, LANES), LANES)].astype(f32)
        return total + block * block

    norm = lax.fori_loop(0, width // LANES, squares, jnp.zeros((orients, LANES), f32))
    norm = 0.5 * jnp.sum(norm, axis=1, keepdims=True)
    diag = lax.broadcasted_iota(jnp.int32, (orients, orients), 0) == lax.broadcasted_iota(jnp.int32, (orients, orients), 1)
    half_norm[...] = jnp.sum(jnp.where(diag, norm, 0.0), axis=0, keepdims=True)

    mass_acc[...] = jnp.zeros_like(mass_acc)

    lane = lax.broadcasted_iota(jnp.int32, (pp, LANES), 1)
    freq = (lane % frame_side - frame_side // 2).astype(f32)
    odd = (lane // frame_side).astype(f32)
    same = lax.broadcasted_iota(jnp.int32, (pp, LANES), 0) == lane
    row8 = lax.broadcasted_iota(jnp.int32, (8, LANES), 0)
    per_block = LANES // frame_side

    def score(k, h):
        q = k * halves + h
        base = q * rows
        at_image = pl.ds(pl.multiple_of(k * per + h * pp, 8), pp)
        a = off_a[at_image, :]
        b = off_b[at_image, :]
        start = turn(a * freq + b * odd)
        step_c, step_s = turn(b * per_block)

        def columns(kb, cs):
            ec, es = cs
            at_r = pl.ds(pl.multiple_of(kb * LANES, LANES), LANES)
            at_i = pl.ds(pl.multiple_of(k_count + kb * LANES, LANES), LANES)
            xr = img_buf[k, pl.ds(h * pp, pp), at_r].astype(f32)
            xi = img_buf[k, pl.ds(h * pp, pp), at_i].astype(f32)
            yr = xr * ec + xi * es
            yi = xi * ec - xr * es
            zr, zi = [None] * SHIFTS, [None] * SHIFTS
            for e in range(SHIFTS // 2):
                c = cos_tab[e:e + 1, at_r]
                d = sin_tab[e:e + 1, at_r]
                rc, rd, ic, id_ = yr * c, yr * d, yi * c, yi * d
                zr[e], zi[e] = rc + id_, ic - rd
                zr[SHIFTS - 1 - e], zi[SHIFTS - 1 - e] = rc - id_, ic + rd
                if (e + 1) % together == 0:
                    for s in (e + 1 - together, SHIFTS - 1 - e):
                        at = pl.ds(pl.multiple_of(base + s * pp, together * pp), together * pp)
                        shifted[at, at_r] = jnp.concatenate(zr[s:s + together], axis=0).astype(bf16)
                        shifted[at, at_i] = jnp.concatenate(zi[s:s + together], axis=0).astype(bf16)
            return ec * step_c - es * step_s, es * step_c + ec * step_s

        lax.fori_loop(0, k_count // LANES, columns, start, unroll=2)
        at = pl.ds(pl.multiple_of(base, rows), rows)
        got = inv_noise * (nt(shifted[at, :], slices[...]) - half_norm[...])
        got = got.reshape(SHIFTS, pp, orients)
        top = jnp.max(jnp.max(got, axis=0), axis=1, keepdims=True)
        term = jnp.exp(got - top[None])
        mass = jnp.sum(jnp.sum(term, axis=0), axis=1, keepdims=True)
        terms[at, :] = term.reshape(rows, orients)
        tops[q] = jnp.broadcast_to(top, (pp, LANES))
        top_row = jnp.sum(jnp.where(same, top, 0.0), axis=0, keepdims=True)
        mass_row = jnp.sum(jnp.where(same, mass, 0.0), axis=0, keepdims=True)
        stats[q, 0] = jnp.where(row8 == 0, top_row, mass_row)
        for i in range(1, n_or):
            stat_copy(q, i).start()

    def stat_copy(q, i):
        return pltpu.make_async_remote_copy(stats.at[q, 0], stats.at[q, i], stat_send.at[q, i], stat_recv.at[q, i],
                                            device_id={"orient": (o + i) % n_or}, device_id_type=MESH)

    def distance(step, c):
        t, h = step // halves, step % halves
        has_left = (t > 0) & (o - t >= 0)
        has_right = (t > 0) & (o + t < n_or)

        @pl.when(has_left)
        def _():
            from_left(t, h).wait_recv()

        @pl.when(has_left & (o < n_or - 1))
        def _():
            to_right(t, h).start()

        @pl.when(has_right)
        def _():
            from_right(t, h).wait_recv()

        @pl.when(has_right & (o > 0))
        def _():
            to_left(t, h).start()

        def side(d, c):
            k = o + t * (2 * d - 1)
            live = (k >= 0) & (k < n_or) & ((t > 0) | (d == 0))

            @pl.when(live)
            def _():
                score(k, h)
            return c

        return lax.fori_loop(0, 2, side, c)


    def collect(step, c):
        k, h = c + step // halves, step % halves
        q = k * halves + h

        def arrive(i, c):
            stat_copy(q, i).wait_recv()
            return c

        lax.fori_loop(1, n_or, arrive, 0)
        every = [stats[q, i] for i in range(n_or)]
        top = functools.reduce(jnp.maximum, [e[0:1] for e in every])
        mass = functools.reduce(jnp.add, [e[1:2] * jnp.exp(e[0:1] - top) for e in every])
        top = jnp.sum(jnp.where(same, top, 0.0), axis=1, keepdims=True)
        mass = jnp.sum(jnp.where(same, mass, 0.0), axis=1, keepdims=True)
        factor = jnp.exp(tops[q][:, 0:1] - top) / mass
        at = pl.ds(pl.multiple_of(q * rows, rows), rows)
        post = terms[at, :].reshape(SHIFTS, pp, orients) * factor[None]
        post = post.reshape(rows, orients).astype(bf16)
        share = nt(hits[...].reshape(seg_count * n_dev, orients), post)
        mass_acc[...] += jnp.broadcast_to(jnp.sum(share, axis=1, keepdims=True), mass_acc.shape)
        shares[:, at] = share.astype(bf16)
        return c

    def gather_in(first, last, fresh):
        lax.fori_loop(0, (last - first) * halves, collect, first)
        lo, hi = first * halves * rows, last * halves * rows
        for p in range(2):
            for j in range(seg_count):
                c0 = p * k_count + j * SEG
                got = jnp.dot(shares[j * n_dev:(j + 1) * n_dev, lo:hi], shifted[lo:hi, c0:c0 + SEG],
                              preferred_element_type=f32)
                acc[p, j] = got if fresh else acc[p, j] + got

    quarter = n_or // 4
    steps = n_or * halves
    early = (n_or - 1) * halves if quarter else steps
    lax.fori_loop(0, early, distance, 0)
    if quarter:
        gather_in(quarter, n_or - quarter, True)
        lax.fori_loop(early, steps, distance, 0)

    load_interp.wait()

    def split(j, c):
        w = interp[j]
        weights[j, :, 0:SEG] = (w >> 4).astype(f32).astype(bf16)
        weights[j, :, SEG:2 * SEG] = (w & 15).astype(f32).astype(bf16)
        return c

    lax.fori_loop(0, seg_count, split, 0)

    if quarter:
        gather_in(0, quarter, False)
        gather_in(n_or - quarter, n_or, False)
    else:
        gather_in(0, n_or, True)

    for j in range(seg_count):
        to = pl.ds(j, n_dev, stride=seg_count)
        for p in range(2):
            for e in range(SEG // LANES):
                by_brick[p * (SEG // LANES) + e, to, :] = acc[p, j, :, e * LANES:(e + 1) * LANES]
        by_brick[2 * SEG // LANES, to, :] = mass_acc[j * n_dev:(j + 1) * n_dev]

    def pack(b, c):
        at = pl.ds(pl.multiple_of(b * seg_count, seg_count), seg_count)
        each = SEG // LANES
        for e in range(each):
            both = jnp.concatenate([by_brick[e, at, :], by_brick[each + e, at, :]], axis=0)
            msg[b, :, e * LANES:(e + 1) * LANES] = both.astype(bf16)
        m = by_brick[2 * each, at, :]
        hi = m.astype(bf16).astype(f32)
        msg[b, :, SEG:SEG + LANES] = jnp.concatenate([hi, m - hi], axis=0).astype(bf16)
        return c

    lax.fori_loop(0, n_dev, pack, 0)

    def msg_copy(i):
        to = (me + i) % n_dev
        return pltpu.make_async_remote_copy(msg.at[to], inbox.at[i], msg_send.at[i], msg_recv.at[i],
                                            device_id=place(to), device_id_type=MESH)

    def post_msg(i, c):
        msg_copy(i).start()
        return c

    lax.fori_loop(1, n_dev, post_msg, 0)

    def take(i, total):
        msg_copy(i).wait_recv()
        return total + inbox[i].astype(f32)

    total = lax.fori_loop(1, n_dev, take, msg[me].astype(f32))
    mass = total[0:seg_count, SEG:] + total[seg_count:, SEG:]
    left = jnp.concatenate([total[:, 0:SEG], jnp.concatenate([mass, mass], axis=1)], axis=0)
    n_rows = 3 * seg_count
    hi = left.astype(bf16).astype(f32)
    both = jnp.concatenate([hi, left - hi], axis=0).astype(bf16)
    place_row = lax.broadcasted_iota(jnp.int32, (n_rows, SEG), 0) % seg_count
    result = jnp.zeros((n_rows, SEG), f32)
    for j in range(seg_count):
        got = jnp.dot(both, weights[j], preferred_element_type=f32)
        got = got[0:n_rows] + got[n_rows:]
        got = got[:, 0:SEG] * (16.0 / 256.0) + got[:, SEG:] * (1.0 / 256.0)
        result = jnp.where(place_row == j, got, result)
    result = jnp.sum(result.reshape(3, seg_count, SEG), axis=1)
    result_out[...] = result

    def settle(step, c):
        t, h = step // halves, step % halves

        @pl.when((o < n_or - 1) & (o - t >= 0))
        def _():
            to_right(t, h).wait_send()

        @pl.when((o > 0) & (o + t < n_or))
        def _():
            to_left(t, h).wait_send()
        return c

    lax.fori_loop(0, (n_or - 1) * halves, settle, 0)

    def settle_stats(q, c):
        for i in range(1, n_or):
            stat_copy(q, i).wait_send()
        return c

    lax.fori_loop(0, n_or * halves, settle_stats, 0)

    def settle_msgs(i, c):
        msg_copy(i).wait_send()
        return c

    lax.fori_loop(1, n_dev, settle_msgs, 0)


def hand_out(result, values_out, weight_out):
    values_out[0] = result[0:2]
    weight_out[...] = result[2:3]


def per_device(images, offsets, slices, seg_map, interp):
    n_or = lax.axis_size("orient")
    n_img = lax.axis_size("img")
    n_brick = lax.axis_size("brick")
    n_dev = n_or * n_img * n_brick
    per, width = images.shape
    k_count = width // 2
    seg_count = k_count // SEG
    orients = slices.shape[0]
    halves = 2 if per % 32 == 0 else 1
    pp = per // halves
    rows = pp * SHIFTS
    pieces = n_or * halves
    coef = np.arange(k_count)
    shift = np.arange(SHIFTS)
    shift = shift[:SHIFTS // 2]
    index = ((shift % 4 - 1.5)[:, None] * (coef % frame_side - frame_side // 2)[None, :]
             + (shift // 4 - 1.5)[:, None] * (coef // frame_side)[None, :])
    angle = 2 * np.pi * index / frame_side
    cos_tab = jnp.asarray(np.cos(angle), f32)
    sin_tab = jnp.asarray(np.sin(angle), f32)
    vmem = pl.BlockSpec(memory_space=pltpu.VMEM)
    hbm = pl.BlockSpec(memory_space=pl.ANY)
    dma = pltpu.SemaphoreType.DMA
    result = pl.pallas_call(
        functools.partial(body, (n_or, n_img, n_brick, halves)),
        out_shape=jax.ShapeDtypeStruct((3, SEG), f32),
        in_specs=[vmem, vmem, hbm, vmem, hbm, vmem, vmem],
        out_specs=vmem,
        scratch_shapes=[
            pltpu.VMEM((n_or, per, width), bf16),
            pltpu.VMEM((orients, width), bf16),
            pltpu.VMEM((seg_count, SEG, SEG), jnp.int32),
            pltpu.VMEM((seg_count, SEG, 2 * SEG), bf16),
            pltpu.VMEM((pieces * rows, width), bf16),
            pltpu.VMEM((pieces * rows, orients), f32),
            pltpu.VMEM((1, orients), f32),
            pltpu.VMEM((seg_count, n_dev, orients), bf16),
            pltpu.VMEM((pieces, pp, LANES), f32),
            pltpu.VMEM((pieces, n_or, 8, LANES), f32),
            pltpu.VMEM((n_dev * seg_count, pieces * rows), bf16),
            pltpu.VMEM((n_or * per, LANES), f32),
            pltpu.VMEM((n_or * per, LANES), f32),
            pltpu.VMEM((2, seg_count, n_dev, SEG), f32),
            pltpu.VMEM((2 * SEG // LANES + 1, n_dev * seg_count, LANES), f32),
            pltpu.VMEM((n_dev * seg_count, LANES), f32),
            pltpu.VMEM((n_dev, 2 * seg_count, SEG + LANES), bf16),
            pltpu.VMEM((n_dev, 2 * seg_count, SEG + LANES), bf16),
            dma((2,)),
            dma((n_or, halves)),
            dma((n_or, halves)),
            dma((n_or + 1, halves)),
            dma((n_or + 1, halves)),
            dma((pieces, n_or)),
            dma((pieces, n_or)),
            dma((n_dev,)),
            dma((n_dev,)),
        ],
        compiler_params=pltpu.CompilerParams(
            collective_id=0, has_side_effects=True, vmem_limit_bytes=56 * 1024 * 1024),
        name="score_and_insert",
    )(images, offsets.T, slices, seg_map.T, interp, cos_tab, sin_tab)
    return pl.pallas_call(
        hand_out,
        out_shape=(jax.ShapeDtypeStruct((1, 2, SEG), f32), jax.ShapeDtypeStruct((1, SEG), f32)),
        in_specs=[vmem],
        out_specs=(vmem, vmem),
        name="hand_out",
    )(result)


def solution(mesh):
    placed = (
        P(("groups", "orient", "img", "brick"), None),
        P("groups", None),
        P(("groups", "orient"), None),
        P(),
        P(("orient", "img", "brick"), None, None, None),
    )
    return jax.shard_map(
        per_device,
        mesh=mesh,
        in_specs=placed,
        out_specs=(
            P(("groups", "orient", "img", "brick"), None, None),
            P(("groups", "orient", "img", "brick"), None),
        ),
        check_vma=False,
    )
```

```python
import functools
import numpy as np
import jax
import jax.numpy as jnp
from jax import lax
from jax.experimental import pallas as pl
from jax.experimental.pallas import tpu as pltpu
from jax.sharding import PartitionSpec as P

SHIFTS = 16
SEG = 256
LANES = 128
frame_side = 64
MESH = pl.DeviceIdType.MESH
f32 = jnp.float32
bf16 = jnp.bfloat16


def turn(index):
    index = index - frame_side * jnp.floor(index * (1.0 / frame_side) + 0.5)
    x = index * f32(np.pi / frame_side)
    y = x * x
    s = x * (1 + y * (-1 / 6 + y * (1 / 120 + y * (-1 / 5040 + y * (1 / 362880 + y * (-1 / 39916800 + y * (1 / 6227020800.0)))))))
    c = 1 + y * (-1 / 2 + y * (1 / 24 + y * (-1 / 720 + y * (1 / 40320 + y * (-1 / 3628800 + y * (1 / 479001600.0))))))
    return 1 - 2 * s * s, 2 * s * c


def nt(a, b):
    return lax.dot_general(a, b, (((1,), (1,)), ((), ())), preferred_element_type=f32)


def body(cfg, images, offs, slices_hbm, seg_map, interp_hbm, cos_tab, sin_tab, result_out,
         img_buf, slices, interp, weights, shifted, terms, half_norm, hits, tops, stats, shares, off_a, off_b, acc, by_brick, mass_acc,
         msg, inbox, load_sem, send_r, send_l, recv_l, recv_r, stat_send, stat_recv, msg_send, msg_recv):
    n_or, n_img, n_brick, halves = cfg
    n_grp = n_img * n_brick
    n_dev = n_or * n_grp
    per, width = images.shape
    k_count = width // 2
    pp = per // halves
    rows = pp * SHIFTS
    together = max(1, 16 // pp)
    seg_count = k_count // SEG
    orients = slices.shape[0]
    inv_noise = 100.0 / k_count
    o = lax.axis_index("orient")
    group = lax.axis_index("img") * n_brick + lax.axis_index("brick")
    me = o * n_grp + group

    def place(flat):
        return {"orient": flat // n_grp, "img": (flat // n_brick) % n_img, "brick": flat % n_brick}

    load_slices = pltpu.make_async_copy(slices_hbm, slices, load_sem.at[0])
    load_interp = pltpu.make_async_copy(interp_hbm.at[0], interp, load_sem.at[1])
    load_slices.start()
    load_interp.start()

    barrier = pltpu.get_barrier_semaphore()

    def greet(i, c):
        pl.semaphore_signal(barrier, inc=1, device_id=place((me + i) % n_dev), device_id_type=MESH)
        return c

    lax.fori_loop(1, n_dev, greet, 0)

    span = SEG // seg_count
    seg_lane = lax.broadcasted_iota(jnp.int32, (seg_count, SEG), 1) % seg_count
    own_j = seg_lane == lax.broadcasted_iota(jnp.int32, (seg_count, SEG), 0)
    src = lax.broadcasted_iota(jnp.int32, (SEG, orients), 0) // seg_count
    dst = lax.broadcasted_iota(jnp.int32, (SEG, orients), 1)

    def regroup(t, total):
        at = pl.ds(pl.multiple_of((o * orients + t * span) * seg_count, SEG), SEG)
        ids = jnp.where(own_j, seg_map[:, at].astype(f32), 0.0).astype(bf16)
        to = jnp.where(src + t * span == dst, 1.0, 0.0).astype(bf16)
        return total + jnp.dot(ids, to, preferred_element_type=f32)

    seg = lax.fori_loop(0, orients // span, regroup, jnp.zeros((seg_count, orients), f32)).astype(jnp.int32)

    image_rows = n_or * per
    picked = lax.broadcasted_iota(jnp.int32, (image_rows, image_rows * n_grp), 0)
    picked = ((picked // per) * n_grp + group) * per + picked % per
    picked = picked == lax.broadcasted_iota(jnp.int32, (image_rows, image_rows * n_grp), 1)
    off = offs[...].astype(f32) - 0.5
    for ref, row in ((off_a, off[0:1]), (off_b, off[1:2])):
        ref[...] = jnp.broadcast_to(jnp.sum(jnp.where(picked, row, 0.0), axis=1, keepdims=True), (image_rows, LANES))

    brick = lax.broadcasted_iota(jnp.int32, (n_dev, orients), 0)
    for j in range(seg_count):
        hits[j] = jnp.where(seg[j:j + 1] == brick, 1.0, 0.0).astype(bf16)

    img_buf[o] = images[...]
    pl.semaphore_wait(barrier, n_dev - 1)

    def part_of(ref, k, h):
        return ref.at[k, pl.ds(h * pp, pp), :]

    def to_right(t, h):
        k = jnp.maximum(o - t, 0)
        ref = part_of(img_buf, k, h)
        return pltpu.make_async_remote_copy(ref, ref, send_r.at[t, h], recv_l.at[t + 1, h],
                                            device_id={"orient": jnp.minimum(o + 1, n_or - 1)}, device_id_type=MESH)

    def to_left(t, h):
        k = jnp.minimum(o + t, n_or - 1)
        ref = part_of(img_buf, k, h)
        return pltpu.make_async_remote_copy(ref, ref, send_l.at[t, h], recv_r.at[t + 1, h],
                                            device_id={"orient": jnp.maximum(o - 1, 0)}, device_id_type=MESH)

    def from_left(t, h):
        ref = part_of(img_buf, jnp.maximum(o - t, 0), h)
        return pltpu.make_async_remote_copy(ref, ref, send_r.at[t, h], recv_l.at[t, h],
                                            device_id={"orient": jnp.maximum(o - 1, 0)}, device_id_type=MESH)

    def from_right(t, h):
        ref = part_of(img_buf, jnp.minimum(o + t, n_or - 1), h)
        return pltpu.make_async_remote_copy(ref, ref, send_l.at[t, h], recv_r.at[t, h],
                                            device_id={"orient": jnp.minimum(o + 1, n_or - 1)}, device_id_type=MESH)

    for h in range(halves):
        @pl.when(o < n_or - 1)
        def _():
            to_right(0, h).start()

        @pl.when(o > 0)
        def _():
            to_left(0, h).start()

    load_slices.wait()

    def squares(b, total):
        block = slices[:, pl.ds(pl.multiple_of(b * LANES, LANES), LANES)].astype(f32)
        return total + block * block

    norm = lax.fori_loop(0, width // LANES, squares, jnp.zeros((orients, LANES), f32))
    norm = 0.5 * jnp.sum(norm, axis=1, keepdims=True)
    diag = lax.broadcasted_iota(jnp.int32, (orients, orients), 0) == lax.broadcasted_iota(jnp.int32, (orients, orients), 1)
    half_norm[...] = jnp.sum(jnp.where(diag, norm, 0.0), axis=0, keepdims=True)

    mass_acc[...] = jnp.zeros_like(mass_acc)

    lane = lax.broadcasted_iota(jnp.int32, (pp, LANES), 1)
    freq = (lane % frame_side - frame_side // 2).astype(f32)
    odd = (lane // frame_side).astype(f32)
    same = lax.broadcasted_iota(jnp.int32, (pp, LANES), 0) == lane
    row8 = lax.broadcasted_iota(jnp.int32, (8, LANES), 0)
    per_block = LANES // frame_side

    def score(k, h):
        q = k * halves + h
        base = q * rows
        at_image = pl.ds(pl.multiple_of(k * per + h * pp, 8), pp)
        a = off_a[at_image, :]
        b = off_b[at_image, :]
        start = turn(a * freq + b * odd)
        step_c, step_s = turn(b * per_block)

        def columns(kb, cs):
            ec, es = cs
            at_r = pl.ds(pl.multiple_of(kb * LANES, LANES), LANES)
            at_i = pl.ds(pl.multiple_of(k_count + kb * LANES, LANES), LANES)
            xr = img_buf[k, pl.ds(h * pp, pp), at_r].astype(f32)
            xi = img_buf[k, pl.ds(h * pp, pp), at_i].astype(f32)
            yr = xr * ec + xi * es
            yi = xi * ec - xr * es
            zr, zi = [None] * SHIFTS, [None] * SHIFTS
            for e in range(SHIFTS // 2):
                c = cos_tab[e:e + 1, at_r]
                d = sin_tab[e:e + 1, at_r]
                rc, rd, ic, id_ = yr * c, yr * d, yi * c, yi * d
                zr[e], zi[e] = rc + id_, ic - rd
                zr[SHIFTS - 1 - e], zi[SHIFTS - 1 - e] = rc - id_, ic + rd
                if (e + 1) % together == 0:
                    for s in (e + 1 - together, SHIFTS - 1 - e):
                        at = pl.ds(pl.multiple_of(base + s * pp, together * pp), together * pp)
                        shifted[at, at_r] = jnp.concatenate(zr[s:s + together], axis=0).astype(bf16)
                        shifted[at, at_i] = jnp.concatenate(zi[s:s + together], axis=0).astype(bf16)
            return ec * step_c - es * step_s, es * step_c + ec * step_s

        lax.fori_loop(0, k_count // LANES, columns, start, unroll=2)
        at = pl.ds(pl.multiple_of(base, rows), rows)
        got = inv_noise * (nt(shifted[at, :], slices[...]) - half_norm[...])
        got = got.reshape(SHIFTS, pp, orients)
        top = jnp.max(jnp.max(got, axis=0), axis=1, keepdims=True)
        term = jnp.exp(got - top[None])
        mass = jnp.sum(jnp.sum(term, axis=0), axis=1, keepdims=True)
        terms[at, :] = term.reshape(rows, orients)
        tops[q] = jnp.broadcast_to(top, (pp, LANES))
        top_row = jnp.sum(jnp.where(same, top, 0.0), axis=0, keepdims=True)
        mass_row = jnp.sum(jnp.where(same, mass, 0.0), axis=0, keepdims=True)
        stats[q, 0] = jnp.where(row8 == 0, top_row, mass_row)
        for i in range(1, n_or):
            stat_copy(q, i).start()

    def stat_copy(q, i):
        return pltpu.make_async_remote_copy(stats.at[q, 0], stats.at[q, i], stat_send.at[q, i], stat_recv.at[q, i],
                                            device_id={"orient": (o + i) % n_or}, device_id_type=MESH)

    steps = n_or * halves
    inner = (o > 0) & (o < n_or - 1)

    def relay(step):
        t, h = step // halves, step % halves
        live = (t > 0) & (t < n_or)
        has_left = live & (o - t >= 0)
        has_right = live & (o + t < n_or)

        @pl.when(has_left)
        def _():
            from_left(t, h).wait_recv()

        @pl.when(has_left & (o < n_or - 1))
        def _():
            to_right(t, h).start()

        @pl.when(has_right)
        def _():
            from_right(t, h).wait_recv()

        @pl.when(has_right & (o > 0))
        def _():
            to_left(t, h).start()

    def distance(step, c):
        t, h = step // halves, step % halves

        def side(d, c):
            @pl.when((d == 0) | (t > 0))
            def _():
                at = jnp.where(t > 0, 2 * step - halves + d, step) + 1
                ahead = jnp.where(inner, at, jnp.where(d == 0, step, steps))

                @pl.when(ahead < steps)
                def _():
                    relay(ahead)

            k = o + t * (2 * d - 1)
            live = (k >= 0) & (k < n_or) & ((t > 0) | (d == 0))

            @pl.when(live)
            def _():
                score(k, h)
            return c

        return lax.fori_loop(0, 2, side, c)

    def collect(step, c):
        k, h = c + step // halves, step % halves
        q = k * halves + h

        def arrive(i, c):
            stat_copy(q, i).wait_recv()
            return c

        lax.fori_loop(1, n_or, arrive, 0)
        every = [stats[q, i] for i in range(n_or)]
        top = functools.reduce(jnp.maximum, [e[0:1] for e in every])
        mass = functools.reduce(jnp.add, [e[1:2] * jnp.exp(e[0:1] - top) for e in every])
        top = jnp.sum(jnp.where(same, top, 0.0), axis=1, keepdims=True)
        mass = jnp.sum(jnp.where(same, mass, 0.0), axis=1, keepdims=True)
        factor = jnp.exp(tops[q][:, 0:1] - top) / mass
        at = pl.ds(pl.multiple_of(q * rows, rows), rows)
        post = terms[at, :].reshape(SHIFTS, pp, orients) * factor[None]
        post = post.reshape(rows, orients).astype(bf16)
        share = nt(hits[...].reshape(seg_count * n_dev, orients), post)
        mass_acc[...] += jnp.broadcast_to(jnp.sum(share, axis=1, keepdims=True), mass_acc.shape)
        shares[:, at] = share.astype(bf16)
        return c

    def gather_in(first, last, fresh):
        lax.fori_loop(0, (last - first) * halves, collect, first)
        lo, hi = first * halves * rows, last * halves * rows
        for p in range(2):
            for j in range(seg_count):
                c0 = p * k_count + j * SEG
                got = jnp.dot(shares[j * n_dev:(j + 1) * n_dev, lo:hi], shifted[lo:hi, c0:c0 + SEG],
                              preferred_element_type=f32)
                acc[p, j] = got if fresh else acc[p, j] + got

    quarter = n_or // 4
    early = (n_or - 1) * halves if quarter else steps
    lax.fori_loop(0, early, distance, 0)
    if quarter:
        gather_in(quarter, n_or - quarter, True)
        lax.fori_loop(early, steps, distance, 0)

    load_interp.wait()

    def split(j, c):
        w = interp[j]
        weights[j, :, 0:SEG] = (w >> 4).astype(f32).astype(bf16)
        weights[j, :, SEG:2 * SEG] = (w & 15).astype(f32).astype(bf16)
        return c

    lax.fori_loop(0, seg_count, split, 0)

    if quarter:
        gather_in(0, quarter, False)
        gather_in(n_or - quarter, n_or, False)
    else:
        gather_in(0, n_or, True)

    for j in range(seg_count):
        to = pl.ds(j, n_dev, stride=seg_count)
        for p in range(2):
            for e in range(SEG // LANES):
                by_brick[p * (SEG // LANES) + e, to, :] = acc[p, j, :, e * LANES:(e + 1) * LANES]
        by_brick[2 * SEG // LANES, to, :] = mass_acc[j * n_dev:(j + 1) * n_dev]

    def pack(b, c):
        at = pl.ds(pl.multiple_of(b * seg_count, seg_count), seg_count)
        each = SEG // LANES
        for e in range(each):
            both = jnp.concatenate([by_brick[e, at, :], by_brick[each + e, at, :]], axis=0)
            msg[b, :, e * LANES:(e + 1) * LANES] = both.astype(bf16)
        m = by_brick[2 * each, at, :]
        hi = m.astype(bf16).astype(f32)
        msg[b, :, SEG:SEG + LANES] = jnp.concatenate([hi, m - hi], axis=0).astype(bf16)
        return c

    lax.fori_loop(0, n_dev, pack, 0)

    def msg_copy(i):
        to = (me + i) % n_dev
        return pltpu.make_async_remote_copy(msg.at[to], inbox.at[i], msg_send.at[i], msg_recv.at[i],
                                            device_id=place(to), device_id_type=MESH)

    def post_msg(i, c):
        msg_copy(i).start()
        return c

    lax.fori_loop(1, n_dev, post_msg, 0)

    def take(i, total):
        msg_copy(i).wait_recv()
        return total + inbox[i].astype(f32)

    total = lax.fori_loop(1, n_dev, take, msg[me].astype(f32))
    mass = total[0:seg_count, SEG:] + total[seg_count:, SEG:]
    left = jnp.concatenate([total[:, 0:SEG], jnp.concatenate([mass, mass], axis=1)], axis=0)
    n_rows = 3 * seg_count
    hi = left.astype(bf16).astype(f32)
    both = jnp.concatenate([hi, left - hi], axis=0).astype(bf16)
    place_row = lax.broadcasted_iota(jnp.int32, (n_rows, SEG), 0) % seg_count
    result = jnp.zeros((n_rows, SEG), f32)
    for j in range(seg_count):
        got = jnp.dot(both, weights[j], preferred_element_type=f32)
        got = got[0:n_rows] + got[n_rows:]
        got = got[:, 0:SEG] * (16.0 / 256.0) + got[:, SEG:] * (1.0 / 256.0)
        result = jnp.where(place_row == j, got, result)
    result = jnp.sum(result.reshape(3, seg_count, SEG), axis=1)
    result_out[...] = result

    def settle(step, c):
        t, h = step // halves, step % halves

        @pl.when((o < n_or - 1) & (o - t >= 0))
        def _():
            to_right(t, h).wait_send()

        @pl.when((o > 0) & (o + t < n_or))
        def _():
            to_left(t, h).wait_send()
        return c

    lax.fori_loop(0, (n_or - 1) * halves, settle, 0)

    def settle_stats(q, c):
        for i in range(1, n_or):
            stat_copy(q, i).wait_send()
        return c

    lax.fori_loop(0, n_or * halves, settle_stats, 0)

    def settle_msgs(i, c):
        msg_copy(i).wait_send()
        return c

    lax.fori_loop(1, n_dev, settle_msgs, 0)


def hand_out(result, values_out, weight_out):
    values_out[0] = result[0:2]
    weight_out[...] = result[2:3]


def per_device(images, offsets, slices, seg_map, interp):
    n_or = lax.axis_size("orient")
    n_img = lax.axis_size("img")
    n_brick = lax.axis_size("brick")
    n_dev = n_or * n_img * n_brick
    per, width = images.shape
    k_count = width // 2
    seg_count = k_count // SEG
    orients = slices.shape[0]
    halves = 2 if per % 32 == 0 else 1
    pp = per // halves
    rows = pp * SHIFTS
    pieces = n_or * halves
    coef = np.arange(k_count)
    shift = np.arange(SHIFTS)
    shift = shift[:SHIFTS // 2]
    index = ((shift % 4 - 1.5)[:, None] * (coef % frame_side - frame_side // 2)[None, :]
             + (shift // 4 - 1.5)[:, None] * (coef // frame_side)[None, :])
    angle = 2 * np.pi * index / frame_side
    cos_tab = jnp.asarray(np.cos(angle), f32)
    sin_tab = jnp.asarray(np.sin(angle), f32)
    vmem = pl.BlockSpec(memory_space=pltpu.VMEM)
    hbm = pl.BlockSpec(memory_space=pl.ANY)
    dma = pltpu.SemaphoreType.DMA
    result = pl.pallas_call(
        functools.partial(body, (n_or, n_img, n_brick, halves)),
        out_shape=jax.ShapeDtypeStruct((3, SEG), f32),
        in_specs=[vmem, vmem, hbm, vmem, hbm, vmem, vmem],
        out_specs=vmem,
        scratch_shapes=[
            pltpu.VMEM((n_or, per, width), bf16),
            pltpu.VMEM((orients, width), bf16),
            pltpu.VMEM((seg_count, SEG, SEG), jnp.int32),
            pltpu.VMEM((seg_count, SEG, 2 * SEG), bf16),
            pltpu.VMEM((pieces * rows, width), bf16),
            pltpu.VMEM((pieces * rows, orients), f32),
            pltpu.VMEM((1, orients), f32),
            pltpu.VMEM((seg_count, n_dev, orients), bf16),
            pltpu.VMEM((pieces, pp, LANES), f32),
            pltpu.VMEM((pieces, n_or, 8, LANES), f32),
            pltpu.VMEM((n_dev * seg_count, pieces * rows), bf16),
            pltpu.VMEM((n_or * per, LANES), f32),
            pltpu.VMEM((n_or * per, LANES), f32),
            pltpu.VMEM((2, seg_count, n_dev, SEG), f32),
            pltpu.VMEM((2 * SEG // LANES + 1, n_dev * seg_count, LANES), f32),
            pltpu.VMEM((n_dev * seg_count, LANES), f32),
            pltpu.VMEM((n_dev, 2 * seg_count, SEG + LANES), bf16),
            pltpu.VMEM((n_dev, 2 * seg_count, SEG + LANES), bf16),
            dma((2,)),
            dma((n_or, halves)),
            dma((n_or, halves)),
            dma((n_or + 1, halves)),
            dma((n_or + 1, halves)),
            dma((pieces, n_or)),
            dma((pieces, n_or)),
            dma((n_dev,)),
            dma((n_dev,)),
        ],
        compiler_params=pltpu.CompilerParams(
            collective_id=0, has_side_effects=True, vmem_limit_bytes=56 * 1024 * 1024),
        name="score_and_insert",
    )(images, offsets.T, slices, seg_map.T, interp, cos_tab, sin_tab)
    return pl.pallas_call(
        hand_out,
        out_shape=(jax.ShapeDtypeStruct((1, 2, SEG), f32), jax.ShapeDtypeStruct((1, SEG), f32)),
        in_specs=[vmem],
        out_specs=(vmem, vmem),
        name="hand_out",
    )(result)


def solution(mesh):
    placed = (
        P(("groups", "orient", "img", "brick"), None),
        P("groups", None),
        P(("groups", "orient"), None),
        P(),
        P(("orient", "img", "brick"), None, None, None),
    )
    return jax.shard_map(
        per_device,
        mesh=mesh,
        in_specs=placed,
        out_specs=(
            P(("groups", "orient", "img", "brick"), None, None),
            P(("groups", "orient", "img", "brick"), None),
        ),
        check_vma=False,
    )
```

```python
import functools
import numpy as np
import jax
import jax.numpy as jnp
from jax import lax
from jax.experimental import pallas as pl
from jax.experimental.pallas import tpu as pltpu
from jax.sharding import PartitionSpec as P

SHIFTS = 16
SEG = 256
LANES = 128
frame_side = 64
MESH = pl.DeviceIdType.MESH
f32 = jnp.float32
bf16 = jnp.bfloat16


def turn(index):
    index = index - frame_side * jnp.floor(index * (1.0 / frame_side) + 0.5)
    x = index * f32(np.pi / frame_side)
    y = x * x
    s = x * (1 + y * (-1 / 6 + y * (1 / 120 + y * (-1 / 5040 + y * (1 / 362880 + y * (-1 / 39916800 + y * (1 / 6227020800.0)))))))
    c = 1 + y * (-1 / 2 + y * (1 / 24 + y * (-1 / 720 + y * (1 / 40320 + y * (-1 / 3628800 + y * (1 / 479001600.0))))))
    return 1 - 2 * s * s, 2 * s * c


def nt(a, b):
    return lax.dot_general(a, b, (((1,), (1,)), ((), ())), preferred_element_type=f32)


def body(cfg, images, offs, slices_hbm, seg_map, interp_hbm, cos_tab, sin_tab, result_out,
         img_buf, slices, slices_t, interp, weights, shifted, terms, half_norm, hits, tops, stats, shares, off_a, off_b, acc, by_brick, mass_acc,
         msg, inbox, load_sem, send_r, send_l, recv_l, recv_r, stat_send, stat_recv, msg_send, msg_recv):
    n_or, n_img, n_brick, halves = cfg
    n_grp = n_img * n_brick
    n_dev = n_or * n_grp
    per, width = images.shape
    k_count = width // 2
    pp = per // halves
    rows = pp * SHIFTS
    together = max(1, 16 // pp)
    seg_count = k_count // SEG
    orients = slices.shape[0]
    inv_noise = 100.0 / k_count
    o = lax.axis_index("orient")
    group = lax.axis_index("img") * n_brick + lax.axis_index("brick")
    me = o * n_grp + group

    def place(flat):
        return {"orient": flat // n_grp, "img": (flat // n_brick) % n_img, "brick": flat % n_brick}

    load_slices = pltpu.make_async_copy(slices_hbm, slices, load_sem.at[0])
    load_interp = pltpu.make_async_copy(interp_hbm.at[0], interp, load_sem.at[1])
    load_slices.start()
    load_interp.start()

    barrier = pltpu.get_barrier_semaphore()

    def greet(i, c):
        pl.semaphore_signal(barrier, inc=1, device_id=place((me + i) % n_dev), device_id_type=MESH)
        return c

    lax.fori_loop(1, n_dev, greet, 0)

    span = SEG // seg_count
    seg_lane = lax.broadcasted_iota(jnp.int32, (seg_count, SEG), 1) % seg_count
    own_j = seg_lane == lax.broadcasted_iota(jnp.int32, (seg_count, SEG), 0)
    src = lax.broadcasted_iota(jnp.int32, (SEG, orients), 0) // seg_count
    dst = lax.broadcasted_iota(jnp.int32, (SEG, orients), 1)

    def regroup(t, total):
        at = pl.ds(pl.multiple_of((o * orients + t * span) * seg_count, SEG), SEG)
        ids = jnp.where(own_j, seg_map[:, at].astype(f32), 0.0).astype(bf16)
        to = jnp.where(src + t * span == dst, 1.0, 0.0).astype(bf16)
        return total + jnp.dot(ids, to, preferred_element_type=f32)

    seg = lax.fori_loop(0, orients // span, regroup, jnp.zeros((seg_count, orients), f32)).astype(jnp.int32)

    image_rows = n_or * per
    picked = lax.broadcasted_iota(jnp.int32, (image_rows, image_rows * n_grp), 0)
    picked = ((picked // per) * n_grp + group) * per + picked % per
    picked = picked == lax.broadcasted_iota(jnp.int32, (image_rows, image_rows * n_grp), 1)
    off = offs[...].astype(f32) - 0.5
    for ref, row in ((off_a, off[0:1]), (off_b, off[1:2])):
        ref[...] = jnp.broadcast_to(jnp.sum(jnp.where(picked, row, 0.0), axis=1, keepdims=True), (image_rows, LANES))

    brick = lax.broadcasted_iota(jnp.int32, (n_dev, orients), 0)
    for j in range(seg_count):
        hits[j] = jnp.where(seg[j:j + 1] == brick, 1.0, 0.0).astype(bf16)

    img_buf[o] = images[...]
    pl.semaphore_wait(barrier, n_dev - 1)

    def part_of(ref, k, h):
        return ref.at[k, pl.ds(h * pp, pp), :]

    def to_right(t, h):
        k = jnp.maximum(o - t, 0)
        ref = part_of(img_buf, k, h)
        return pltpu.make_async_remote_copy(ref, ref, send_r.at[t, h], recv_l.at[t + 1, h],
                                            device_id={"orient": jnp.minimum(o + 1, n_or - 1)}, device_id_type=MESH)

    def to_left(t, h):
        k = jnp.minimum(o + t, n_or - 1)
        ref = part_of(img_buf, k, h)
        return pltpu.make_async_remote_copy(ref, ref, send_l.at[t, h], recv_r.at[t + 1, h],
                                            device_id={"orient": jnp.maximum(o - 1, 0)}, device_id_type=MESH)

    def from_left(t, h):
        ref = part_of(img_buf, jnp.maximum(o - t, 0), h)
        return pltpu.make_async_remote_copy(ref, ref, send_r.at[t, h], recv_l.at[t, h],
                                            device_id={"orient": jnp.maximum(o - 1, 0)}, device_id_type=MESH)

    def from_right(t, h):
        ref = part_of(img_buf, jnp.minimum(o + t, n_or - 1), h)
        return pltpu.make_async_remote_copy(ref, ref, send_l.at[t, h], recv_r.at[t, h],
                                            device_id={"orient": jnp.minimum(o + 1, n_or - 1)}, device_id_type=MESH)

    for h in range(halves):
        @pl.when(o < n_or - 1)
        def _():
            to_right(0, h).start()

        @pl.when(o > 0)
        def _():
            to_left(0, h).start()

    load_slices.wait()

    def squares(b, total):
        at = pl.ds(pl.multiple_of(b * LANES, LANES), LANES)
        block = slices[:, at].astype(f32).T
        slices_t[at, :] = block.astype(bf16)
        return total + jnp.sum((block * block).reshape(LANES // 8, 8, orients), axis=0)

    norm = lax.fori_loop(0, width // LANES, squares, jnp.zeros((8, orients), f32))
    half_norm[...] = 0.5 * jnp.sum(norm, axis=0, keepdims=True)

    mass_acc[...] = jnp.zeros_like(mass_acc)

    lane = lax.broadcasted_iota(jnp.int32, (pp, LANES), 1)
    freq = (lane % frame_side - frame_side // 2).astype(f32)
    odd = (lane // frame_side).astype(f32)
    same = lax.broadcasted_iota(jnp.int32, (pp, LANES), 0) == lane
    row8 = lax.broadcasted_iota(jnp.int32, (8, LANES), 0)
    per_block = LANES // frame_side

    def score(k, h):
        q = k * halves + h
        base = q * rows
        at_image = pl.ds(pl.multiple_of(k * per + h * pp, 8), pp)
        a = off_a[at_image, :]
        b = off_b[at_image, :]
        start = turn(a * freq + b * odd)
        step_c, step_s = turn(b * per_block)

        def columns(kb, cs):
            ec, es = cs
            at_r = pl.ds(pl.multiple_of(kb * LANES, LANES), LANES)
            at_i = pl.ds(pl.multiple_of(k_count + kb * LANES, LANES), LANES)
            xr = img_buf[k, pl.ds(h * pp, pp), at_r].astype(f32)
            xi = img_buf[k, pl.ds(h * pp, pp), at_i].astype(f32)
            yr = xr * ec + xi * es
            yi = xi * ec - xr * es
            zr, zi = [None] * SHIFTS, [None] * SHIFTS
            for e in range(SHIFTS // 2):
                c = cos_tab[e:e + 1, at_r]
                d = sin_tab[e:e + 1, at_r]
                rc, rd, ic, id_ = yr * c, yr * d, yi * c, yi * d
                zr[e], zi[e] = rc + id_, ic - rd
                zr[SHIFTS - 1 - e], zi[SHIFTS - 1 - e] = rc - id_, ic + rd
                if (e + 1) % together == 0:
                    for s in (e + 1 - together, SHIFTS - 1 - e):
                        at = pl.ds(pl.multiple_of(base + s * pp, together * pp), together * pp)
                        shifted[at, at_r] = jnp.concatenate(zr[s:s + together], axis=0).astype(bf16)
                        shifted[at, at_i] = jnp.concatenate(zi[s:s + together], axis=0).astype(bf16)
            return ec * step_c - es * step_s, es * step_c + ec * step_s

        lax.fori_loop(0, k_count // LANES, columns, start, unroll=2)
        at = pl.ds(pl.multiple_of(base, rows), rows)
        got = inv_noise * (jnp.dot(shifted[at, :], slices_t[...], preferred_element_type=f32) - half_norm[...])
        got = got.reshape(SHIFTS, pp, orients)
        top = jnp.max(jnp.max(got, axis=0), axis=1, keepdims=True)
        term = jnp.exp(got - top[None])
        mass = jnp.sum(jnp.sum(term, axis=0), axis=1, keepdims=True)
        terms[at, :] = term.reshape(rows, orients)
        tops[q] = jnp.broadcast_to(top, (pp, LANES))
        top_row = jnp.sum(jnp.where(same, top, 0.0), axis=0, keepdims=True)
        mass_row = jnp.sum(jnp.where(same, mass, 0.0), axis=0, keepdims=True)
        stats[q, 0] = jnp.where(row8 == 0, top_row, mass_row)
        for i in range(1, n_or):
            stat_copy(q, i).start()

    def stat_copy(q, i):
        return pltpu.make_async_remote_copy(stats.at[q, 0], stats.at[q, i], stat_send.at[q, i], stat_recv.at[q, i],
                                            device_id={"orient": (o + i) % n_or}, device_id_type=MESH)

    steps = n_or * halves
    inner = (o > 0) & (o < n_or - 1)

    def relay(step):
        t, h = step // halves, step % halves
        live = (t > 0) & (t < n_or)
        has_left = live & (o - t >= 0)
        has_right = live & (o + t < n_or)

        @pl.when(has_left)
        def _():
            from_left(t, h).wait_recv()

        @pl.when(has_left & (o < n_or - 1))
        def _():
            to_right(t, h).start()

        @pl.when(has_right)
        def _():
            from_right(t, h).wait_recv()

        @pl.when(has_right & (o > 0))
        def _():
            to_left(t, h).start()

    def distance(step, c):
        t, h = step // halves, step % halves

        def side(d, c):
            @pl.when((d == 0) | (t > 0))
            def _():
                at = jnp.where(t > 0, 2 * step - halves + d, step) + 1
                ahead = jnp.where(inner, at, jnp.where(d == 0, step, steps))

                @pl.when(ahead < steps)
                def _():
                    relay(ahead)

            k = o + t * (2 * d - 1)
            live = (k >= 0) & (k < n_or) & ((t > 0) | (d == 0))

            @pl.when(live)
            def _():
                score(k, h)
            return c

        return lax.fori_loop(0, 2, side, c)

    def collect(step, c):
        k, h = c + step // halves, step % halves
        q = k * halves + h

        def arrive(i, c):
            stat_copy(q, i).wait_recv()
            return c

        lax.fori_loop(1, n_or, arrive, 0)
        every = [stats[q, i] for i in range(n_or)]
        top = functools.reduce(jnp.maximum, [e[0:1] for e in every])
        mass = functools.reduce(jnp.add, [e[1:2] * jnp.exp(e[0:1] - top) for e in every])
        top = jnp.sum(jnp.where(same, top, 0.0), axis=1, keepdims=True)
        mass = jnp.sum(jnp.where(same, mass, 0.0), axis=1, keepdims=True)
        factor = jnp.exp(tops[q][:, 0:1] - top) / mass
        at = pl.ds(pl.multiple_of(q * rows, rows), rows)
        post = terms[at, :].reshape(SHIFTS, pp, orients) * factor[None]
        post = post.reshape(rows, orients).astype(bf16)
        share = nt(hits[...].reshape(seg_count * n_dev, orients), post)
        mass_acc[...] += jnp.broadcast_to(jnp.sum(share, axis=1, keepdims=True), mass_acc.shape)
        shares[:, at] = share.astype(bf16)
        return c

    def gather_in(first, last, fresh):
        lax.fori_loop(0, (last - first) * halves, collect, first)
        lo, hi = first * halves * rows, last * halves * rows
        for p in range(2):
            for j in range(seg_count):
                c0 = p * k_count + j * SEG
                got = jnp.dot(shares[j * n_dev:(j + 1) * n_dev, lo:hi], shifted[lo:hi, c0:c0 + SEG],
                              preferred_element_type=f32)
                acc[p, j] = got if fresh else acc[p, j] + got

    quarter = n_or // 4
    early = (n_or - 1) * halves if quarter else steps
    lax.fori_loop(0, early, distance, 0)
    if quarter:
        gather_in(quarter, n_or - quarter, True)
        lax.fori_loop(early, steps, distance, 0)

    load_interp.wait()

    def split(j, c):
        w = interp[j]
        weights[j, :, 0:SEG] = (w >> 4).astype(f32).astype(bf16)
        weights[j, :, SEG:2 * SEG] = (w & 15).astype(f32).astype(bf16)
        return c

    lax.fori_loop(0, seg_count, split, 0)

    if quarter:
        gather_in(0, quarter, False)
        gather_in(n_or - quarter, n_or, False)
    else:
        gather_in(0, n_or, True)

    for j in range(seg_count):
        to = pl.ds(j, n_dev, stride=seg_count)
        for p in range(2):
            for e in range(SEG // LANES):
                by_brick[p * (SEG // LANES) + e, to, :] = acc[p, j, :, e * LANES:(e + 1) * LANES]
        by_brick[2 * SEG // LANES, to, :] = mass_acc[j * n_dev:(j + 1) * n_dev]

    def pack(b, c):
        at = pl.ds(pl.multiple_of(b * seg_count, seg_count), seg_count)
        each = SEG // LANES
        for e in range(each):
            both = jnp.concatenate([by_brick[e, at, :], by_brick[each + e, at, :]], axis=0)
            msg[b, :, e * LANES:(e + 1) * LANES] = both.astype(bf16)
        m = by_brick[2 * each, at, :]
        hi = m.astype(bf16).astype(f32)
        msg[b, :, SEG:SEG + LANES] = jnp.concatenate([hi, m - hi], axis=0).astype(bf16)
        return c

    lax.fori_loop(0, n_dev, pack, 0)

    def msg_copy(i):
        to = (me + i) % n_dev
        return pltpu.make_async_remote_copy(msg.at[to], inbox.at[i], msg_send.at[i], msg_recv.at[i],
                                            device_id=place(to), device_id_type=MESH)

    def post_msg(i, c):
        msg_copy(i).start()
        return c

    lax.fori_loop(1, n_dev, post_msg, 0)

    def take(i, total):
        msg_copy(i).wait_recv()
        return total + inbox[i].astype(f32)

    total = lax.fori_loop(1, n_dev, take, msg[me].astype(f32))
    mass = total[0:seg_count, SEG:] + total[seg_count:, SEG:]
    left = jnp.concatenate([total[:, 0:SEG], jnp.concatenate([mass, mass], axis=1)], axis=0)
    n_rows = 3 * seg_count
    hi = left.astype(bf16).astype(f32)
    both = jnp.concatenate([hi, left - hi], axis=0).astype(bf16)
    place_row = lax.broadcasted_iota(jnp.int32, (n_rows, SEG), 0) % seg_count
    result = jnp.zeros((n_rows, SEG), f32)
    for j in range(seg_count):
        got = jnp.dot(both, weights[j], preferred_element_type=f32)
        got = got[0:n_rows] + got[n_rows:]
        got = got[:, 0:SEG] * (16.0 / 256.0) + got[:, SEG:] * (1.0 / 256.0)
        result = jnp.where(place_row == j, got, result)
    result = jnp.sum(result.reshape(3, seg_count, SEG), axis=1)
    result_out[...] = result

    def settle(step, c):
        t, h = step // halves, step % halves

        @pl.when((o < n_or - 1) & (o - t >= 0))
        def _():
            to_right(t, h).wait_send()

        @pl.when((o > 0) & (o + t < n_or))
        def _():
            to_left(t, h).wait_send()
        return c

    lax.fori_loop(0, (n_or - 1) * halves, settle, 0)

    def settle_stats(q, c):
        for i in range(1, n_or):
            stat_copy(q, i).wait_send()
        return c

    lax.fori_loop(0, n_or * halves, settle_stats, 0)

    def settle_msgs(i, c):
        msg_copy(i).wait_send()
        return c

    lax.fori_loop(1, n_dev, settle_msgs, 0)


def hand_out(result, values_out, weight_out):
    values_out[0] = result[0:2]
    weight_out[...] = result[2:3]


def per_device(images, offsets, slices, seg_map, interp):
    n_or = lax.axis_size("orient")
    n_img = lax.axis_size("img")
    n_brick = lax.axis_size("brick")
    n_dev = n_or * n_img * n_brick
    per, width = images.shape
    k_count = width // 2
    seg_count = k_count // SEG
    orients = slices.shape[0]
    halves = 2 if per % 32 == 0 else 1
    pp = per // halves
    rows = pp * SHIFTS
    pieces = n_or * halves
    coef = np.arange(k_count)
    shift = np.arange(SHIFTS)
    shift = shift[:SHIFTS // 2]
    index = ((shift % 4 - 1.5)[:, None] * (coef % frame_side - frame_side // 2)[None, :]
             + (shift // 4 - 1.5)[:, None] * (coef // frame_side)[None, :])
    angle = 2 * np.pi * index / frame_side
    cos_tab = jnp.asarray(np.cos(angle), f32)
    sin_tab = jnp.asarray(np.sin(angle), f32)
    vmem = pl.BlockSpec(memory_space=pltpu.VMEM)
    hbm = pl.BlockSpec(memory_space=pl.ANY)
    dma = pltpu.SemaphoreType.DMA
    result = pl.pallas_call(
        functools.partial(body, (n_or, n_img, n_brick, halves)),
        out_shape=jax.ShapeDtypeStruct((3, SEG), f32),
        in_specs=[vmem, vmem, hbm, vmem, hbm, vmem, vmem],
        out_specs=vmem,
        scratch_shapes=[
            pltpu.VMEM((n_or, per, width), bf16),
            pltpu.VMEM((orients, width), bf16),
            pltpu.VMEM((width, orients), bf16),
            pltpu.VMEM((seg_count, SEG, SEG), jnp.int32),
            pltpu.VMEM((seg_count, SEG, 2 * SEG), bf16),
            pltpu.VMEM((pieces * rows, width), bf16),
            pltpu.VMEM((pieces * rows, orients), f32),
            pltpu.VMEM((1, orients), f32),
            pltpu.VMEM((seg_count, n_dev, orients), bf16),
            pltpu.VMEM((pieces, pp, LANES), f32),
            pltpu.VMEM((pieces, n_or, 8, LANES), f32),
            pltpu.VMEM((n_dev * seg_count, pieces * rows), bf16),
            pltpu.VMEM((n_or * per, LANES), f32),
            pltpu.VMEM((n_or * per, LANES), f32),
            pltpu.VMEM((2, seg_count, n_dev, SEG), f32),
            pltpu.VMEM((2 * SEG // LANES + 1, n_dev * seg_count, LANES), f32),
            pltpu.VMEM((n_dev * seg_count, LANES), f32),
            pltpu.VMEM((n_dev, 2 * seg_count, SEG + LANES), bf16),
            pltpu.VMEM((n_dev, 2 * seg_count, SEG + LANES), bf16),
            dma((2,)),
            dma((n_or, halves)),
            dma((n_or, halves)),
            dma((n_or + 1, halves)),
            dma((n_or + 1, halves)),
            dma((pieces, n_or)),
            dma((pieces, n_or)),
            dma((n_dev,)),
            dma((n_dev,)),
        ],
        compiler_params=pltpu.CompilerParams(
            collective_id=0, has_side_effects=True, vmem_limit_bytes=56 * 1024 * 1024),
        name="score_and_insert",
    )(images, offsets.T, slices, seg_map.T, interp, cos_tab, sin_tab)
    return pl.pallas_call(
        hand_out,
        out_shape=(jax.ShapeDtypeStruct((1, 2, SEG), f32), jax.ShapeDtypeStruct((1, SEG), f32)),
        in_specs=[vmem],
        out_specs=(vmem, vmem),
        name="hand_out",
    )(result)


def solution(mesh):
    placed = (
        P(("groups", "orient", "img", "brick"), None),
        P("groups", None),
        P(("groups", "orient"), None),
        P(),
        P(("orient", "img", "brick"), None, None, None),
    )
    return jax.shard_map(
        per_device,
        mesh=mesh,
        in_specs=placed,
        out_specs=(
            P(("groups", "orient", "img", "brick"), None, None),
            P(("groups", "orient", "img", "brick"), None),
        ),
        check_vma=False,
    )
```
